256 devices in a mesh: expert: 64 (over z, y, core), seq: 4 (over x).
Axes of the slice: x: 4, y: 4, z: 8, core: 2. Of those that a mesh axis runs over, the one named last changes fastest.
Arguments:
- routes: int32 [32768, 10], P(('expert', 'seq')), may hold values from 0 to 63, all different within a row; in each aligned block of 128 rows (0 to 127, 128 to 255, ...) at most 30 rows name the same one
- combine_weights: float32 [32768, 10], P(('expert', 'seq')), may hold values from 0.02 to 0.5
- expert_rows: bfloat16 [64, 4, 64, 30, 1024], P('expert', 'seq'), may hold values from -6 to 6
- expert_weight: bfloat16 [64, 1024, 2048], P('expert'), may hold values from -0.1875 to 0.1875
- conv_grad: bfloat16 [32768, 4096], P(('expert', 'seq')), may hold values from -6 to 6
- conv_input: bfloat16 [32768, 4096], P(('expert', 'seq')), may hold values from -6 to 6
- conv_weight: float32 [4, 4096], P(None, 'seq'), may hold values from -2.5 to 2.5
Outputs:
- token_grad: bfloat16 [32768, 2048], P(('expert', 'seq'))
- input_grad: bfloat16 [32768, 4096], P('expert', 'seq')
- weight_grad: float32 [4, 4096], P(None, 'seq')
The draws below stay inside these ranges and needn't reach their ends.
Inputs may be any that keep to these rules, and one draw needn't show every extreme that they name: `routes`: each row names 10 different experts. In each aligned block of 128 rows (the tokens of one device) no expert is named by more than 30 rows, a bound that some block reaches.
All inputs are finite; a program needn't handle non-finite values.
Results may differ from the reference program's by a relative error of at most 0.0049.
Values may be sent and summed in bfloat16 or wider, within the bound.
No kernel may reach another device: no remote copies, remote signals or barrier semaphores. Data moves between devices by JAX's collectives and lax.ppermute only.
A program may use at most 128 MiB of HBM per device.

```python
import math
import jax
import jax.numpy as jnp
import numpy as np
from jax import lax

D = 2048
FFE = 512
CONV = 4096
TAPS = 4
TOK_DEV = 128
EXPERTS = 64
TOP = 10
CAP = 30
TOKENS = 32768
N_EXPERT = 64
N_SEQ = 4


def block_scale(key, shape, split, smallest, high):
    level, own = 1.0, jax.random.fold_in(key, 6)
    for dim, blocks in split:
        draws = jnp.exp(jax.random.uniform(jax.random.fold_in(own, dim), (blocks,), jnp.float32, smallest / len(split), high / len(split)))
        level = level * jnp.repeat(draws, shape[dim] // blocks).reshape([-1 if axis == dim else 1 for axis in range(len(shape))])
    return level


def routed_block(key, own, number, rows, number_of, top, bound, skew):
    sequence = jax.random.permutation(key, number_of)
    heavy_load, ordinary = portions_of(number_of, rows * top, bound, skew, True), portions_of(number_of, rows * top, bound, skew, False)
    places = jnp.arange(number_of)

    def named(lengths, offset_by):
        used = int((lengths > 0).sum())
        fixed = max(1, used // 4)
        moved = fixed + (places - fixed + offset_by * (used - fixed)) % max(1, number_of - fixed)
        return jnp.zeros((number_of,), jnp.int32).at[sequence[jnp.where(places < fixed, places, moved)]].set(jnp.asarray(lengths, jnp.int32))

    lengths = jnp.where(number % 4 == 0, named(heavy_load, number // 4), named(ordinary, number - number // 4 - 1))
    mixed = jax.random.permutation(jax.random.fold_in(own, 3), number_of)
    source_of, receiver = mixed[0:number_of // 2 * 2:2], mixed[1:number_of // 2 * 2:2]
    slack = jnp.minimum(lengths[source_of] - 1, bound - lengths[receiver]) // 2
    slack = jnp.where((source_of == sequence[0]) | (receiver == sequence[0]) | (lengths[receiver] == 0), 0, jnp.maximum(slack, 0))
    moved = jax.random.randint(jax.random.fold_in(own, 4), (number_of // 2,), 0, 1 << 20) % (slack + 1)
    lengths = lengths.at[source_of].add(-moved).at[receiver].add(moved)
    items = jnp.searchsorted(jnp.cumsum(lengths), jnp.arange(rows * top), side="right").astype(jnp.int32)
    listing = items.reshape(top, rows).T
    listing = listing[jax.random.permutation(jax.random.fold_in(own, 1), rows)]
    offset_by = jax.random.randint(jax.random.fold_in(own, 2), (rows, 1), 0, top)
    return jnp.take_along_axis(listing, (jnp.arange(top)[None, :] + offset_by) % top, axis=1)


def portions_of(amount, total, most, slope, full):
    loads = [(1 << 20) // math.isqrt(grade ** slope) + 1 for grade in range(1, amount + 1)]
    largest = most if full else min(most, max(-(-total // amount), total * loads[0] // sum(loads)))
    least = 1 if total - largest >= amount - 1 else 0
    counts, rest = [largest] + [least] * (amount - 1), total - largest - least * (amount - 1)
    while rest > 0:
        movable = [i for i in range(1, amount) if counts[i] < largest] or [i for i in range(1, amount) if counts[i] < most]
        pool, left = sum([loads[i] for i in movable]), rest
        for i in movable:
            more = min(most - counts[i], max(1, left * loads[i] // pool), rest)
            counts[i] = counts[i] + more
            rest = rest - more
    return np.array(counts)


def gaussian(own_key, extent, spread, limit, cuts=(), kind=jnp.bfloat16):
    values = jax.random.normal(own_key, extent, jnp.float32) * spread
    if len(cuts) > 0:
        values = block_scale(own_key, extent, cuts, -0.22, 0.18) * values
    return jnp.clip(values, min=-limit, max=limit).astype(kind)


def setup_inputs(seed: int = 0) -> dict:
    key_of = jax.random.split(jax.random.key(seed), 8)
    routes_keys = jax.random.split(jax.random.fold_in(key_of[0], 1), TOKENS // TOK_DEV)
    routes_turns = jax.random.permutation(jax.random.fold_in(key_of[0], 3), TOKENS // TOK_DEV)
    routes = jax.vmap(lambda own, number: routed_block(jax.random.fold_in(key_of[0], 2), own, number, TOK_DEV, EXPERTS, TOP, CAP, 2))(routes_keys, routes_turns).reshape((TOKENS, TOP))
    combine_weights = jnp.clip(jnp.exp(math.log(0.5) - 3.218876 * jax.random.uniform(key_of[1], (TOKENS, TOP), jnp.float32) ** block_scale(key_of[1], (TOKENS, TOP), ((0, 256),), -0.2, 0.2)), 0.02, 0.5)
    expert_rows = gaussian(key_of[2], (EXPERTS, N_SEQ, N_EXPERT, CAP, 2 * FFE), 1.0, 6.0, ((0, 64), (1, 4)))
    expert_weight = gaussian(key_of[3], (EXPERTS, 2 * FFE, D), (2 * FFE) ** -0.5, 0.1875, ((0, 64),))
    conv_grad = gaussian(key_of[4], (TOKENS, CONV), 1.0, 6.0, ((0, 256),))
    conv_input = gaussian(key_of[5], (TOKENS, CONV), 1.0, 6.0, ((0, 256),))
    conv_weight = gaussian(key_of[6], (TAPS, CONV), 0.5, 2.5, ((1, 4),), jnp.float32)
    return dict(routes=routes, combine_weights=combine_weights, expert_rows=expert_rows, expert_weight=expert_weight, conv_grad=conv_grad, conv_input=conv_input, conv_weight=conv_weight)


def slot_table(routes):
    blocks = routes.shape[0] // TOK_DEV
    flat_routes = routes.reshape(blocks, TOK_DEV * TOP)
    labels = jnp.arange(EXPERTS, dtype=jnp.int32)
    onehot = (flat_routes[:, :, None] == labels[None, None, :]).astype(jnp.int32)
    rank_table = jnp.cumsum(onehot, axis=1) - onehot
    return lax.optimization_barrier(jnp.sum(rank_table * onehot, axis=2)).reshape(routes.shape[0], TOP)

def reference(routes, combine_weights, expert_rows, expert_weight, conv_grad, conv_input, conv_weight):
    slot_index = slot_table(routes)
    block_id = jnp.arange(TOKENS, dtype=jnp.int32) // TOK_DEV
    source_seq = block_id % N_SEQ
    source_group = block_id // N_SEQ

    def add_expert(expert_id, summed):
        rows_in = lax.dynamic_index_in_dim(expert_rows, expert_id, 0, keepdims=False)
        weight_now = lax.dynamic_index_in_dim(expert_weight, expert_id, 0, keepdims=False)
        expert_out = jnp.dot(rows_in.reshape(-1, 2 * FFE), weight_now, preferred_element_type=jnp.float32)
        expert_out = expert_out.astype(jnp.bfloat16).reshape(N_SEQ, N_EXPERT, CAP, D)
        hit = routes == expert_id
        slot_now = lax.optimization_barrier(jnp.sum(jnp.where(hit, slot_index, 0), axis=1)).astype(jnp.int32)
        gate_now = lax.optimization_barrier(jnp.sum(jnp.where(hit, combine_weights, jnp.float32(0.0)), axis=1))
        picked = expert_out[source_seq, source_group, slot_now]
        return summed + gate_now[:, None] * picked.astype(jnp.float32)
    summed = lax.fori_loop(0, EXPERTS, add_expert, jnp.zeros((TOKENS, D), jnp.float32))
    token_grad = summed.astype(jnp.bfloat16)
    reach = TAPS - 1
    input_pad = jnp.pad(conv_input.astype(jnp.float32), ((reach, reach), (0, 0)))
    pre_act = jnp.zeros((TOKENS, CONV), jnp.float32)
    for offset in range(TAPS):
        pre_act = pre_act + conv_weight[offset][None, :] * input_pad[offset:offset + TOKENS]
    sigmoid = 1.0 / (1.0 + jnp.exp(-pre_act))
    pre_grad = conv_grad.astype(jnp.float32) * sigmoid * (1.0 + pre_act * (1.0 - sigmoid))
    grad_pad = jnp.pad(pre_grad, ((0, reach), (0, 0)))
    input_grad = jnp.zeros((TOKENS, CONV), jnp.float32)
    taps_list = []
    for offset in range(TAPS):
        input_grad = input_grad + conv_weight[offset][None, :] * grad_pad[reach - offset:reach - offset + TOKENS]
        taps_list.append(lax.optimization_barrier(jnp.sum(pre_grad * input_pad[offset:offset + TOKENS], axis=0)))
    weight_grad = jnp.stack(taps_list, axis=0) * (1.0 / math.sqrt(TOKENS))
    return (token_grad, input_grad.astype(jnp.bfloat16), weight_grad)
```

```python
import math

import jax
import jax.numpy as jnp
from jax import lax
from jax.experimental import pallas as pl
from jax.experimental.pallas import tpu as pltpu
from jax.sharding import PartitionSpec as P

NZ, NY, NC = 8, 4, 2
CHUNKS = 4
BF = jnp.bfloat16
F32 = jnp.float32


def device_at(z, y, c):
    return (z * NY + y) * NC + c


def shift(value, dz=0, dy=0, dc=0):
    pairs = [
        (device_at(z, y, c), device_at((z + dz) % NZ, (y + dy) % NY, (c + dc) % NC))
        for z in range(NZ)
        for y in range(NY)
        for c in range(NC)
    ]
    return lax.ppermute(value, "expert", pairs)


def from_behind(value, axis, steps):
    count = lax.axis_size(axis)
    leading, last = (max(0, -steps), min(count, count - steps))
    return lax.ppermute(value, axis, [(source, source + steps) for source in range(leading, last)])


def conv_core(grad_rows, input_rows, input_past, grad_next, input_next, kernel):
    reach = kernel.shape[0] - 1
    count = grad_rows.shape[0]
    input_ext = jnp.concatenate([input_past, input_rows, input_next], axis=0).astype(F32)
    grad_ext = jnp.concatenate([grad_rows, grad_next], axis=0).astype(F32)
    pre_act = jnp.zeros(grad_ext.shape, F32)
    for offset in range(reach + 1):
        pre_act = pre_act + kernel[offset][None, :] * input_ext[offset : offset + count + reach]
    sigmoid = 1.0 / (1.0 + jnp.exp(-pre_act))
    pre_grad = grad_ext * sigmoid * (1.0 + pre_act * (1.0 - sigmoid))
    result = jnp.zeros(grad_rows.shape, F32)
    taps_list = []
    for offset in range(reach + 1):
        result = (
            result + kernel[offset][None, :] * pre_grad[reach - offset : reach - offset + count]
        )
        taps_list.append(jnp.sum(pre_grad[:count] * input_ext[offset : offset + count], axis=0))
    return (result.astype(BF), jnp.stack(taps_list, axis=0))


def conv_part(conv_grad, conv_input, conv_weight, tokens_total):
    reach = conv_weight.shape[0] - 1
    scale = 1.0 / math.sqrt(tokens_total)
    grad_rows, input_rows = (
        lax.all_to_all(conv_grad, "seq", split_axis=1, concat_axis=0, tiled=True),
        lax.all_to_all(conv_input, "seq", split_axis=1, concat_axis=0, tiled=True),
    )
    input_past = from_behind(input_rows[-reach:], "expert", 1)
    front = jnp.stack([grad_rows[:reach], input_rows[:reach]], axis=0)
    front_next = from_behind(front, "expert", -1)
    input_grad, taps = conv_core(
        grad_rows, input_rows, input_past, front_next[0], front_next[1], conv_weight
    )
    taps = taps + shift(taps, dc=1)
    c_taps = taps
    taps = flip_sum(c_taps, lambda z, y, c: (z, y ^ 1, c))
    taps = flip_sum(taps, lambda z, y, c: (z, y ^ 2, c))
    taps = flip_sum(taps, lambda z, y, c: (z ^ 1, y, c))
    taps = flip_sum(taps, lambda z, y, c: (z ^ 2, y, c))
    taps = flip_sum(taps, lambda z, y, c: (z ^ 4, y, c))
    return input_grad, taps * scale


def flip_sum(value, partner):
    pairs = [
        (device_at(z, y, c), device_at(*partner(z, y, c)))
        for z in range(NZ)
        for y in range(NY)
        for c in range(NC)
    ]
    return value + lax.ppermute(value, "expert", pairs)


def sort_kernel(order_ref, rows_ref, out_ref):
    order = order_ref[...]
    parts = out_ref.shape[0]
    for group in range(rows_ref.shape[0]):
        moved = jnp.dot(order, rows_ref[group], preferred_element_type=F32).astype(BF)
        out_ref[:, group] = moved.reshape(parts, moved.shape[0] // parts, moved.shape[1])


def sort_rows(rows, y, c):
    capacity, groups, depth = rows.shape
    parts = NY * NC
    size = 2 * groups
    count = capacity // 2
    rows = rows.reshape(count, size, depth)
    place = lax.broadcasted_iota(jnp.int32, (size, size), 0)
    source = lax.broadcasted_iota(jnp.int32, (size, size), 1)
    part, inner = place // (2 * NZ), place % (2 * NZ)
    core, row = (c + part // NY) % NC, (y + part % NY) % NY
    wanted = (inner // NZ) * groups + (inner % NZ) * parts + row * NC + core
    order = (source == wanted).astype(BF)
    step = 5 if count % 5 == 0 else 1
    out = pl.pallas_call(
        sort_kernel,
        grid=(count // step,),
        in_specs=[
            pl.BlockSpec((size, size), lambda i: (0, 0)),
            pl.BlockSpec((step, size, depth), lambda i: (i, 0, 0)),
        ],
        out_specs=pl.BlockSpec((parts, step, size // parts, depth), lambda i: (0, i, 0, 0)),
        out_shape=jax.ShapeDtypeStruct((parts, count, size // parts, depth), BF),
        compiler_params=pltpu.CompilerParams(vmem_limit_bytes=32 * 1024 * 1024),
    )(order, rows)
    return out.reshape(parts * count * (size // parts), depth)


def combine_matrix(routes, weights, capacity, z, y, c):
    top, tokens = routes.shape
    info = jnp.concatenate([routes.astype(F32), weights], axis=0)[None]
    info = jnp.concatenate([info, shift(info, dz=-1)], axis=0)
    info = jnp.concatenate([info, shift(info, dz=-2)], axis=0)
    info = jnp.concatenate([info, shift(info, dz=-4)], axis=0)
    named, gates = info[:, :top], info[:, top:]
    part = jnp.arange(NY * NC, dtype=jnp.int32)
    expert = device_at(z, (y - part // NC + NY) % NY, (c + part % NC) % NC).astype(F32)
    hit = named[None] == expert[:, None, None, None]
    gate = jnp.sum(jnp.where(hit, gates[None], 0.0), axis=2)
    mask = jnp.any(hit, axis=2).astype(BF)
    before = jnp.triu(jnp.ones((tokens, tokens), BF), 1)
    slot = jnp.dot(mask.reshape(-1, tokens), before, preferred_element_type=F32)
    slot = slot.reshape(NY * NC, NZ * tokens)
    gate = gate.reshape(NY * NC, NZ * tokens)
    width = NY * NC * capacity * NZ
    lane = jnp.arange(width, dtype=jnp.int32)
    spread = (lane[None] // (capacity * NZ) == part[:, None]).astype(BF)

    def expand(value):
        return lax.dot_general(
            value.astype(BF), spread, (((0,), (0,)), ((), ())), preferred_element_type=F32
        )

    high = gate.astype(BF)
    low = (gate - high.astype(F32)).astype(BF)
    toward = (z + jnp.arange(NZ * tokens, dtype=jnp.int32) // tokens) % NZ
    chosen = (expand(slot) == ((lane // NZ) % capacity).astype(F32)[None]) & (
        toward[:, None] == (lane % NZ)[None]
    )
    return jnp.concatenate(
        [
            jnp.where(chosen, expand(high), 0.0).astype(BF),
            jnp.where(chosen, expand(low), 0.0).astype(BF),
        ],
        axis=1,
    )


def z_ring(part):
    half = part.shape[2] // 2
    ahead = shift(part[4, :, :half].astype(BF), dz=1)
    back = shift(part[4, :, half:].astype(BF), dz=-1)
    zeros = jnp.zeros_like(ahead)
    ahead = jnp.concatenate([ahead, zeros], axis=1)
    back = jnp.concatenate([zeros, back], axis=1)
    for apart in (3, 2, 1):
        ahead = shift((part[apart] + ahead.astype(F32)).astype(BF), dz=1)
        back = shift((part[NZ - apart] + back.astype(F32)).astype(BF), dz=-1)
    return (part[0] + ahead.astype(F32) + back.astype(F32)).astype(BF)


def expert_part(routes, combine_weights, expert_rows, expert_weight):
    me = lax.axis_index("expert")
    z, y, c = me // (NY * NC), (me // NC) % NY, me % NC
    capacity = expert_rows.shape[3]
    tokens = routes.shape[0]
    width = expert_weight.shape[2]
    rows = jnp.transpose(expert_rows[0, 0], (1, 0, 2))
    rows = sort_rows(rows, y, c)
    matrix = combine_matrix(routes.T, combine_weights.T, capacity, z, y, c)
    block = capacity * NZ
    half = NY * block
    columns = width // CHUNKS
    results = []
    for chunk in range(CHUNKS):
        weight = expert_weight[0, :, chunk * columns : (chunk + 1) * columns]
        out = jnp.dot(rows, weight, preferred_element_type=F32).astype(BF)
        other = shift(out[half:], dc=1)
        arrived = []
        for apart in range(NY):
            place = slice(apart * block, (apart + 1) * block)
            both = jnp.concatenate([out[place], other[place]], axis=0)
            arrived.append(shift(both, dy=apart) if apart else both)
        stacked = jnp.concatenate(arrived + arrived, axis=0)
        part = jnp.dot(matrix, stacked, preferred_element_type=F32)
        results.append(z_ring(part.reshape(NZ, tokens, columns)))
    return jnp.concatenate(results, axis=1)


def local(routes, combine_weights, expert_rows, expert_weight, conv_grad, conv_input, conv_weight):
    tokens_total = routes.shape[0] * lax.axis_size("expert") * lax.axis_size("seq")
    token_grad = expert_part(routes, combine_weights, expert_rows, expert_weight)
    input_grad, weight_grad = conv_part(conv_grad, conv_input, conv_weight, tokens_total)
    return (token_grad, input_grad, weight_grad)


def solution(mesh):
    placed = (
        P(("expert", "seq"), None),
        P(("expert", "seq"), None),
        P("expert", "seq", None, None, None),
        P("expert", None, None),
        P(("expert", "seq"), None),
        P(("expert", "seq"), None),
        P(None, "seq"),
    )
    return jax.shard_map(
        local,
        mesh=mesh,
        in_specs=placed,
        out_specs=(P(("expert", "seq"), None), P("expert", "seq"), P(None, "seq")),
        check_vma=False,
    )
```

```python
import functools
import math

import jax
import jax.numpy as jnp
from jax import lax
from jax.experimental import pallas as pl
from jax.experimental.pallas import tpu as pltpu
from jax.sharding import PartitionSpec as P

NZ, NY, NC = 8, 4, 2
WIDTHS = (1024, 1024)
OVERLAP = 2
PACKED = {1152: 384, 896: 896, 1280: 640, 768: 384, 1024: 512}
BF = jnp.bfloat16
F32 = jnp.float32
VMEM = 40 * 1024 * 1024
LARGE = 58 * 1024 * 1024
QUICK = pl.CostEstimate(flops=0, bytes_accessed=0, transcendentals=0)


def device_at(z, y, c):
    return (z * NY + y) * NC + c


def shift(value, dz=0, dy=0, dc=0):
    pairs = [
        (device_at(z, y, c), device_at((z + dz) % NZ, (y + dy) % NY, (c + dc) % NC))
        for z in range(NZ)
        for y in range(NY)
        for c in range(NC)
    ]
    return lax.ppermute(value, "expert", pairs)


def after(value, *first):
    return lax.optimization_barrier((value, *first))[0]


def from_behind(value, axis, steps):
    count = lax.axis_size(axis)
    leading, last = (max(0, -steps), min(count, count - steps))
    return lax.ppermute(value, axis, [(source, source + steps) for source in range(leading, last)])


def conv_kernel(grad_ref, input_ref, taps_ref, result_ref, sums_ref):
    count, reach = result_ref.shape[0], taps_ref.shape[0] - 1
    inputs = input_ref[...].astype(F32)
    near = [inputs[offset : offset + count + reach] for offset in range(reach + 1)]
    taps = [taps_ref[offset : offset + 1] for offset in range(reach + 1)]
    pre_act = taps[0] * near[0]
    for offset in range(1, reach + 1):
        pre_act = pre_act + taps[offset] * near[offset]
    sigmoid = 1.0 / (1.0 + jnp.exp(-pre_act))
    pre_grad = grad_ref[...].astype(F32) * sigmoid * (1.0 + pre_act * (1.0 - sigmoid))
    result = taps[0] * pre_grad[reach : reach + count]
    for offset in range(1, reach + 1):
        result = result + taps[offset] * pre_grad[reach - offset : reach - offset + count]
    result_ref[...] = result.astype(BF)
    here = pre_grad[:count]
    sums = [jnp.sum(here * near[o][:count], axis=0, keepdims=True) for o in range(reach + 1)]
    sums_ref[...] = jnp.concatenate(sums, axis=0)


def conv_core(grad_rows, input_rows, input_past, grad_next, input_next, kernel):
    count, channels = grad_rows.shape
    taps = kernel.shape[0]
    tile = 256
    input_ext = jnp.concatenate([input_past, input_rows, input_next], axis=0)
    grad_ext = jnp.concatenate([grad_rows, grad_next], axis=0)
    column = lambda i: (0, i)
    return pl.pallas_call(
        conv_kernel,
        grid=(channels // tile,),
        in_specs=[
            pl.BlockSpec((grad_ext.shape[0], tile), column),
            pl.BlockSpec((input_ext.shape[0], tile), column),
            pl.BlockSpec((taps, tile), column),
        ],
        out_specs=[pl.BlockSpec((count, tile), column), pl.BlockSpec((taps, tile), column)],
        out_shape=[
            jax.ShapeDtypeStruct((count, channels), BF),
            jax.ShapeDtypeStruct((taps, channels), F32),
        ],
        compiler_params=pltpu.CompilerParams(vmem_limit_bytes=VMEM),
        cost_estimate=QUICK,
        name="conv",
    )(grad_ext, input_ext, kernel)


def conv_edges(conv_grad, conv_input, conv_weight):
    reach = conv_weight.shape[0] - 1
    with jax.named_scope("convedges"):
        input_past = from_behind(conv_input[-reach:], ("expert", "seq"), 1)
        front = jnp.stack([conv_grad[:reach], conv_input[:reach]], axis=0)
        front_next = from_behind(front, ("expert", "seq"), -1)
    with jax.named_scope("convtaps"):
        count = lax.axis_size("seq")
        kernel = jnp.broadcast_to(conv_weight[None], (count, *conv_weight.shape))
        kernel = lax.all_to_all(kernel, "seq", split_axis=0, concat_axis=0, tiled=True)
        kernel = jnp.concatenate([kernel[i] for i in range(count)], axis=1)
    return input_past, front_next, kernel


def conv_local(conv_grad, conv_input, edges):
    input_past, front_next, kernel = edges
    with jax.named_scope("convcore"):
        return conv_core(conv_grad, conv_input, input_past, front_next[0], front_next[1], kernel)


def conv_rest(result, taps):
    count = lax.axis_size("seq")
    width = taps.shape[1] // count
    with jax.named_scope("convmove"):
        result = lax.all_to_all(result, "seq", split_axis=1, concat_axis=0, tiled=True)
    with jax.named_scope("tapsmove"):
        taps = jnp.stack([taps[:, i * width : (i + 1) * width] for i in range(count)])
        taps = lax.all_to_all(taps, "seq", split_axis=0, concat_axis=0, tiled=True)
        return result, jnp.sum(taps, axis=0)


PARTNERS = (
    lambda z, y, c: (z, y, c ^ 1),
    lambda z, y, c: (z ^ 1, y, c),
    lambda z, y, c: (z ^ 2, y, c),
    lambda z, y, c: (z ^ 4, y, c),
    lambda z, y, c: (z, y ^ 1, c),
    lambda z, y, c: (z, y ^ 2, c),
)


def flip_sum(value, partner):
    pairs = [
        (device_at(z, y, c), device_at(*partner(z, y, c)))
        for z in range(NZ)
        for y in range(NY)
        for c in range(NC)
    ]
    return value + lax.ppermute(value, "expert", pairs)


def sort_kernel(order_ref, rows_ref, out_ref):
    order = order_ref[...]
    parts = out_ref.shape[0]
    for group in range(rows_ref.shape[0]):
        moved = jnp.dot(order, rows_ref[group], preferred_element_type=F32).astype(BF)
        out_ref[:, group] = moved.reshape(parts, moved.shape[0] // parts, moved.shape[1])


def sort_rows(rows, y, c):
    capacity, groups, depth = rows.shape
    parts = NY * NC
    size = 2 * groups
    count = capacity // 2
    rows = rows.reshape(count, size, depth)
    place = lax.broadcasted_iota(jnp.int32, (size, size), 0)
    source = lax.broadcasted_iota(jnp.int32, (size, size), 1)
    part, inner = place // (2 * NZ), place % (2 * NZ)
    core, row = (c + part // NY) % NC, (y + part % NY) % NY
    wanted = (inner // NZ) * groups + (inner % NZ) * parts + row * NC + core
    order = (source == wanted).astype(BF)
    step = 5 if count % 5 == 0 else 1
    out = pl.pallas_call(
        sort_kernel,
        grid=(count // step,),
        in_specs=[
            pl.BlockSpec((size, size), lambda i: (0, 0)),
            pl.BlockSpec((step, size, depth), lambda i: (i, 0, 0)),
        ],
        out_specs=pl.BlockSpec((parts, step, size // parts, depth), lambda i: (0, i, 0, 0)),
        out_shape=jax.ShapeDtypeStruct((parts, count, size // parts, depth), BF),
        compiler_params=pltpu.CompilerParams(vmem_limit_bytes=VMEM),
        cost_estimate=QUICK,
        name="sort",
    )(order, rows)
    return out.reshape(parts * count * (size // parts), depth)


def turned(info, experts):
    top, tokens = info.shape[0] // 2, info.shape[1]
    named, gates = info[:top], info[top:]
    rows, marks = [], []
    for expert in experts:
        hit = named == expert.astype(F32)
        rows.append(jnp.sum(jnp.where(hit, gates, 0.0), axis=0, keepdims=True))
        marks.append(jnp.sum(jnp.where(hit, 1.0, 0.0), axis=0, keepdims=True))
    gate, mark = jnp.concatenate(rows, axis=0), jnp.concatenate(marks, axis=0)
    down = lax.broadcasted_iota(jnp.int32, (tokens, tokens), 0)
    along = lax.broadcasted_iota(jnp.int32, (tokens, tokens), 1)
    same = jnp.where(down == along, 1.0, 0.0).astype(BF)
    before = jnp.where(along < down, 1.0, 0.0).astype(BF)

    def turn(matrix, value):
        return lax.dot_general(
            matrix, value, (((1,), (1,)), ((), ())), preferred_element_type=F32
        )

    return turn(same, gate.astype(BF)), turn(before, mark.astype(BF))


def put_gates(out_ref, at, lanes, columns, picks, lane_slot):
    gate, slot = columns

    def chosen(value):
        result = value[:, picks[-1] : picks[-1] + 1]
        for lane, pick in reversed(list(zip(lanes, picks[:-1], strict=True))):
            result = jnp.where(lane, value[:, pick : pick + 1], result)
        return result

    here = chosen(slot) == lane_slot
    out_ref[at] = jnp.where(here, chosen(gate), 0.0).astype(BF)


def own_lanes(pair, goal):
    lane = lax.broadcasted_iota(jnp.int32, (1, pair), 1)
    first = lane < pair // NC
    inner = jnp.where(first, lane, lane - pair // NC)
    return first, jnp.where(inner % NZ == goal, inner // NZ, -1).astype(F32)


def position(me):
    return me // (NY * NC), (me // NC) % NY, me % NC


def column_kernel(order, me_ref, info_ref, out_ref):
    sources, _, pair = out_ref.shape
    tokens = info_ref.shape[2]
    z, y, c = position(me_ref[0])
    experts = [
        device_at(z, (y + NY - behind) % NY, (c + core) % NC)
        for behind in ROWS_FROM
        for core in range(NC)
    ]
    for number, place in enumerate(order):
        columns = turned(info_ref[place], experts)
        first, lane_slot = own_lanes(pair, (z + place) % NZ)
        for source in range(sources):
            picks = (NC * source, NC * source + 1)
            at = (source, slice(number * tokens, (number + 1) * tokens), slice(None))
            put_gates(out_ref, at, [first], columns, picks, lane_slot)


def column_matrix(me, info, order, capacity):
    tokens = info.shape[2]
    sources, pair = len(ROWS_FROM), NC * capacity * NZ
    return pl.pallas_call(
        functools.partial(column_kernel, order),
        grid_spec=pltpu.PrefetchScalarGridSpec(
            num_scalar_prefetch=1,
            grid=(1,),
            in_specs=[pl.BlockSpec(info.shape, lambda i, p: (0, 0, 0))],
            out_specs=pl.BlockSpec((sources, len(order) * tokens, pair), lambda i, p: (0, 0, 0)),
        ),
        out_shape=jax.ShapeDtypeStruct((sources, len(order) * tokens, pair), BF),
        compiler_params=pltpu.CompilerParams(vmem_limit_bytes=VMEM),
        cost_estimate=QUICK,
        name="gatescolumn",
    )(me.reshape(1), info)


def multiply_kernel(rows_ref, weight_ref, out_ref):
    out_ref[...] = jnp.dot(rows_ref[...], weight_ref[0], preferred_element_type=F32).astype(BF)


def multiply_half(rows, weight, half, start, columns):
    size, depth = rows.shape[0] // 2, rows.shape[1]
    tile = 256 if start % 256 == 0 and columns % 256 == 0 else 128
    return pl.pallas_call(
        multiply_kernel,
        grid=(columns // tile,),
        in_specs=[
            pl.BlockSpec((size, depth), lambda i: (half, 0)),
            pl.BlockSpec((1, depth, tile), lambda i: (0, 0, start // tile + i)),
        ],
        out_specs=pl.BlockSpec((size, tile), lambda i: (0, i)),
        out_shape=jax.ShapeDtypeStruct((size, columns), BF),
        compiler_params=pltpu.CompilerParams(vmem_limit_bytes=LARGE),
        cost_estimate=QUICK,
        name="multiply",
    )(rows, weight)


def pack_kernel(kept_ref, other_ref, *out_refs):
    block = out_refs[0].shape[0] // NC
    for part, ref in enumerate(out_refs):
        ref[:block] = kept_ref[part * block : (part + 1) * block]
        ref[block:] = other_ref[part * block : (part + 1) * block]


def pack(kept, other):
    size, columns = kept.shape
    tile, pair = PACKED[columns], NC * size // NY
    return pl.pallas_call(
        pack_kernel,
        grid=(columns // tile,),
        in_specs=[pl.BlockSpec((size, tile), lambda i: (0, i))] * 2,
        out_specs=[pl.BlockSpec((pair, tile), lambda i: (0, i))] * NY,
        out_shape=[jax.ShapeDtypeStruct((pair, columns), BF)] * NY,
        compiler_params=pltpu.CompilerParams(vmem_limit_bytes=VMEM),
        cost_estimate=QUICK,
        name="pack",
    )(kept, other)


def merge_kernel(matrix_ref, *refs):
    rows, out_ref = refs[:-1], refs[-1]
    total = None
    for part, ref in enumerate(rows):
        term = jnp.dot(matrix_ref[part], ref[...], preferred_element_type=F32)
        total = term if total is None else total + term
    out_ref[...] = total.astype(out_ref.dtype)


def merge_rows(matrix, rows, dtype, steps):
    sources, places, depth = matrix.shape
    columns = rows[0].shape[1]
    step = places // steps
    return pl.pallas_call(
        merge_kernel,
        grid=(steps,),
        in_specs=[pl.BlockSpec((sources, step, depth), lambda i: (0, i, 0))]
        + [pl.BlockSpec((depth, columns), lambda i: (0, 0))] * sources,
        out_specs=pl.BlockSpec((step, columns), lambda i: (i, 0)),
        out_shape=jax.ShapeDtypeStruct((places, columns), dtype),
        compiler_params=pltpu.CompilerParams(vmem_limit_bytes=LARGE if steps > 1 else VMEM),
        cost_estimate=QUICK,
        name="merge",
    )(matrix, *rows)


def z_ring(four, rest, gate):
    half = four.shape[1] // 2
    ahead = shift(four[:, :half], dz=1)
    back = shift(four[:, half:], dz=-1)
    zeros = jnp.zeros_like(ahead)
    ahead = jnp.concatenate([ahead, zeros], axis=1)
    back = jnp.concatenate([zeros, back], axis=1)

    def part(apart):
        return rest[ORDER.index(apart)]

    for apart in (3, 2, 1):
        ahead, back = gate(4 - apart, ahead, back)
        ahead = shift((part(apart) + ahead.astype(F32)).astype(BF), dz=1)
        back = shift((part(NZ - apart) + back.astype(F32)).astype(BF), dz=-1)
    return (part(0) + ahead.astype(F32) + back.astype(F32)).astype(BF)


ROWS_FROM = (0, 1, 3, 2)
ORDER = (3, 5, 2, 6, 1, 7, 0)
BEHIND = (0, -1, 1, -2, 2)


def expert_part(
    routes,
    combine_weights,
    expert_rows,
    expert_weight,
    conv_grad,
    conv_input,
    conv_weight,
    tokens_total,
):
    me = lax.axis_index("expert")
    z, y, c = me // (NY * NC), (me // NC) % NY, me % NC
    capacity = expert_rows.shape[3]
    tokens, top = routes.shape
    block = capacity * NZ
    half = NY * block

    with jax.named_scope("sort"):
        rows = jnp.transpose(expert_rows[0, 0], (1, 0, 2))
        rows = sort_rows(rows, y, c)

    starts = [sum(WIDTHS[:chunk]) for chunk in range(len(WIDTHS))]
    def ready(chunk, rows_now):
        place = (starts[chunk], WIDTHS[chunk])
        weight = expert_weight[0, :, place[0] : sum(place)]
        with jax.named_scope(f"multiply{chunk}"):
            if chunk:
                out = multiply_half(rows_now, expert_weight, 1, *place)
                kept = multiply_half(after(rows_now, out), expert_weight, 0, *place)
            else:
                out = jnp.dot(rows_now[half:], weight, preferred_element_type=F32).astype(BF)
                kept = after(rows_now, out)[:half]
                kept = jnp.dot(kept, weight, preferred_element_type=F32).astype(BF)
        with jax.named_scope(f"swap{chunk}"):
            other = shift(out, dc=1)
        with jax.named_scope(f"pack{chunk}"):
            return pack(kept, other), out

    with jax.named_scope("info"):
        column = jnp.concatenate([routes.T.astype(F32), combine_weights.T], axis=0)[None]
        column = after(column, rows)
        column = jnp.concatenate([column, shift(column, dz=-1)], axis=0)

    def exchange(chunk, parts):
        with jax.named_scope(f"rows{chunk}"):
            return [parts[0]] + [shift(parts[apart], dy=apart) for apart in ROWS_FROM[1:]]

    count = len(WIDTHS)
    parts_first, out = ready(0, rows)
    parts = [parts_first]
    arrived = [exchange(0, parts[0])]
    begin = parts[0][1:]
    edges = conv_edges(
        after(conv_grad, *begin), after(conv_input, *begin), after(conv_weight, rows)
    )
    with jax.named_scope("info"):
        column = after(column, *parts[0][1:])
        for apart in (2, 4):
            column = jnp.concatenate([column, shift(column, dz=-apart)], axis=0)
    with jax.named_scope("gatescolumn"):
        matrix_four = column_matrix(me, column, (4,), capacity)
        matrix_rest = column_matrix(me, column, ORDER, capacity)
    result, taps = conv_local(conv_grad, conv_input, edges)
    for chunk in range(1, count):
        parts.append(ready(chunk, after(rows, *parts[-1][1:]))[0])
        waited = [*arrived[chunk - 1][1:], matrix_rest, result, taps]
        arrived.append(exchange(chunk, [after(part, *waited) for part in parts[chunk]]))
    input_grad, taps = conv_rest(after(result, *arrived[0][1:]), after(taps, *arrived[0][1:]))

    results, progress = [], [None] * count
    for chunk in range(count):
        slots_now = arrived[chunk]
        last = chunk + 1 == count
        if not last:
            slots_now = [after(value, *parts[chunk + 1][1:]) for value in slots_now]
        if chunk >= 1:
            slots_now = [after(value, progress[chunk - 1]) for value in slots_now]

        def gate(step, ahead, back):
            first = []
            if step == OVERLAP:
                progress[chunk] = ahead
            if not last and step == 2:
                first += [*arrived[chunk + 1][1:], taps_at[1], input_grad]
            return [after(value, *first) for value in (ahead, back)] if first else (ahead, back)

        with jax.named_scope(f"merge{chunk}"):
            four = merge_rows(matrix_four, slots_now, BF, 1)
            slots_now = [after(value, four) for value in slots_now]
            rest = merge_rows(matrix_rest, slots_now, F32, 2)
            rest = rest.reshape(NZ - 1, tokens, WIDTHS[chunk])
        if chunk == 0:
            taps_at = [taps]
            for number, partner in enumerate(PARTNERS):
                with jax.named_scope(f"taps{number}"):
                    taps_at.append(flip_sum(taps_at[-1], partner))
        with jax.named_scope(f"ring{chunk}"):
            results.append(z_ring(four, rest, gate))
    weight_grad = taps_at[-1] * (1.0 / math.sqrt(tokens_total))
    return jnp.concatenate(results, axis=1), input_grad, weight_grad


def local(routes, combine_weights, expert_rows, expert_weight, conv_grad, conv_input, conv_weight):
    tokens_total = routes.shape[0] * lax.axis_size("expert") * lax.axis_size("seq")
    return expert_part(
        routes,
        combine_weights,
        expert_rows,
        expert_weight,
        conv_grad,
        conv_input,
        conv_weight,
        tokens_total,
    )


def solution(mesh):
    placed = (
        P(("expert", "seq"), None),
        P(("expert", "seq"), None),
        P("expert", "seq", None, None, None),
        P("expert", None, None),
        P(("expert", "seq"), None),
        P(("expert", "seq"), None),
        P(None, "seq"),
    )
    return jax.shard_map(
        local,
        mesh=mesh,
        in_specs=placed,
        out_specs=(P(("expert", "seq"), None), P("expert", "seq"), P(None, "seq")),
        check_vma=False,
    )
```

```python
import functools
import math

import jax
import jax.numpy as jnp
from jax import lax
from jax.experimental import pallas as pl
from jax.experimental.pallas import tpu as pltpu
from jax.sharding import PartitionSpec as P

NZ, NY, NC = 8, 4, 2
REACH = 3
WIDTHS = (1024, 1024)
BF = jnp.bfloat16
F32 = jnp.float32
VMEM = 40 * 1024 * 1024
LARGE = 58 * 1024 * 1024
QUICK = pl.CostEstimate(flops=0, bytes_accessed=0, transcendentals=0)


def device_at(z, y, c):
    return (z * NY + y) * NC + c


def shift(value, dz=0, dy=0, dc=0):
    pairs = [
        (device_at(z, y, c), device_at((z + dz) % NZ, (y + dy) % NY, (c + dc) % NC))
        for z in range(NZ)
        for y in range(NY)
        for c in range(NC)
    ]
    return lax.ppermute(value, "expert", pairs)


def after(value, *first):
    return lax.optimization_barrier((value, *first))[0]


def from_behind(value, axis, steps):
    count = lax.axis_size(axis)
    leading, last = (max(0, -steps), min(count, count - steps))
    return lax.ppermute(value, axis, [(source, source + steps) for source in range(leading, last)])


def conv_kernel(grad_ref, input_ref, taps_ref, result_ref, sums_ref):
    count, reach = result_ref.shape[0], taps_ref.shape[0] - 1
    inputs = input_ref[...].astype(F32)
    near = [inputs[offset : offset + count + reach] for offset in range(reach + 1)]
    taps = [taps_ref[offset : offset + 1] for offset in range(reach + 1)]
    pre_act = taps[0] * near[0]
    for offset in range(1, reach + 1):
        pre_act = pre_act + taps[offset] * near[offset]
    sigmoid = 1.0 / (1.0 + jnp.exp(-pre_act))
    pre_grad = grad_ref[...].astype(F32) * sigmoid * (1.0 + pre_act * (1.0 - sigmoid))
    result = taps[0] * pre_grad[reach : reach + count]
    for offset in range(1, reach + 1):
        result = result + taps[offset] * pre_grad[reach - offset : reach - offset + count]
    result_ref[...] = result.astype(BF)
    here = pre_grad[:count]
    sums = [jnp.sum(here * near[o][:count], axis=0, keepdims=True) for o in range(reach + 1)]
    sums_ref[...] = jnp.concatenate(sums, axis=0)


def conv_core(grad_rows, input_rows, input_past, grad_next, input_next, kernel):
    count, channels = grad_rows.shape
    taps = kernel.shape[0]
    tile = 256
    input_ext = jnp.concatenate([input_past, input_rows, input_next], axis=0)
    grad_ext = jnp.concatenate([grad_rows, grad_next], axis=0)
    column = lambda i: (0, i)
    return pl.pallas_call(
        conv_kernel,
        grid=(channels // tile,),
        in_specs=[
            pl.BlockSpec((grad_ext.shape[0], tile), column),
            pl.BlockSpec((input_ext.shape[0], tile), column),
            pl.BlockSpec((taps, tile), column),
        ],
        out_specs=[pl.BlockSpec((count, tile), column), pl.BlockSpec((taps, tile), column)],
        out_shape=[
            jax.ShapeDtypeStruct((count, channels), BF),
            jax.ShapeDtypeStruct((taps, channels), F32),
        ],
        compiler_params=pltpu.CompilerParams(vmem_limit_bytes=VMEM),
        cost_estimate=QUICK,
        name="conv",
    )(grad_ext, input_ext, kernel)


def conv_edges(conv_grad, conv_input):
    with jax.named_scope("convedges"):
        past = from_behind(conv_input[-REACH:], ("expert", "seq"), 1)
        front = jnp.stack([conv_grad[:REACH], conv_input[:REACH]], axis=0)
        return past, from_behind(front, ("expert", "seq"), -1)


def conv_taps(conv_weight):
    count = lax.axis_size("seq")
    with jax.named_scope("convtaps"):
        kernel = jnp.broadcast_to(conv_weight[None], (count, *conv_weight.shape))
        kernel = lax.all_to_all(kernel, "seq", split_axis=0, concat_axis=0, tiled=True)
        return jnp.concatenate([kernel[i] for i in range(count)], axis=1)


def conv_local(conv_grad, conv_input, edges, kernel):
    past, front = edges
    with jax.named_scope("convcore"):
        result, taps = conv_core(conv_grad, conv_input, past, front[0], front[1], kernel)
    return result, taps


def taps_move(taps):
    count = lax.axis_size("seq")
    with jax.named_scope("tapsmove"):
        width = taps.shape[1] // count
        taps = jnp.stack([taps[:, i * width : (i + 1) * width] for i in range(count)])
        taps = lax.all_to_all(taps, "seq", split_axis=0, concat_axis=0, tiled=True)
        return jnp.sum(taps, axis=0)


def keep_kernel(value_ref, out_ref):
    out_ref[...] = value_ref[...]


def conv_move(result):
    with jax.named_scope("convmove"):
        result = lax.all_to_all(result, "seq", split_axis=1, concat_axis=0, tiled=True)
        rows, columns = result.shape
        block = pl.BlockSpec((rows // 4, columns), lambda i: (i, 0))
        return pl.pallas_call(
            keep_kernel,
            grid=(4,),
            in_specs=[block],
            out_specs=block,
            out_shape=jax.ShapeDtypeStruct(result.shape, BF),
            cost_estimate=QUICK,
            name="keep",
        )(result)


PARTNERS = (
    lambda z, y, c: (z, y, c ^ 1),
    lambda z, y, c: (z ^ 4, y, c),
    lambda z, y, c: (z ^ 2, y, c),
    lambda z, y, c: (z ^ 1, y, c),
    lambda z, y, c: (z, y ^ 1, c),
    lambda z, y, c: (z, y ^ 2, c),
)


def flip_sum(value, partner):
    pairs = [
        (device_at(z, y, c), device_at(*partner(z, y, c)))
        for z in range(NZ)
        for y in range(NY)
        for c in range(NC)
    ]
    return value + lax.ppermute(value, "expert", pairs)


def sort_kernel(order_ref, rows_ref, out_ref):
    order = order_ref[...]
    parts = out_ref.shape[0]
    for group in range(rows_ref.shape[0]):
        moved = jnp.dot(order, rows_ref[group], preferred_element_type=F32).astype(BF)
        out_ref[:, group] = moved.reshape(parts, moved.shape[0] // parts, moved.shape[1])


def sort_rows(rows, y, c):
    capacity, groups, depth = rows.shape
    parts = NY * NC
    size = 2 * groups
    count = capacity // 2
    rows = rows.reshape(count, size, depth)
    place = lax.broadcasted_iota(jnp.int32, (size, size), 0)
    source = lax.broadcasted_iota(jnp.int32, (size, size), 1)
    part, inner = place // (2 * NZ), place % (2 * NZ)
    core, row = (c + part // NY) % NC, (y + part % NY) % NY
    wanted = (inner // NZ) * groups + (inner % NZ) * parts + row * NC + core
    order = (source == wanted).astype(BF)
    step = 5 if count % 5 == 0 else 1
    out = pl.pallas_call(
        sort_kernel,
        grid=(count // step,),
        in_specs=[
            pl.BlockSpec((size, size), lambda i: (0, 0)),
            pl.BlockSpec((step, size, depth), lambda i: (i, 0, 0)),
        ],
        out_specs=pl.BlockSpec((parts, step, size // parts, depth), lambda i: (0, i, 0, 0)),
        out_shape=jax.ShapeDtypeStruct((parts, count, size // parts, depth), BF),
        compiler_params=pltpu.CompilerParams(vmem_limit_bytes=VMEM),
        cost_estimate=QUICK,
        name="sort",
    )(order, rows)
    return out.reshape(parts * count * (size // parts), depth)


def turned(info, experts):
    top, tokens = info.shape[0] // 2, info.shape[1]
    named, gates = info[:top], info[top:]
    rows, marks = [], []
    for expert in experts:
        hit = named == expert.astype(F32)
        rows.append(jnp.sum(jnp.where(hit, gates, 0.0), axis=0, keepdims=True))
        marks.append(jnp.sum(jnp.where(hit, 1.0, 0.0), axis=0, keepdims=True))
    gate, mark = jnp.concatenate(rows, axis=0), jnp.concatenate(marks, axis=0)
    down = lax.broadcasted_iota(jnp.int32, (tokens, tokens), 0)
    along = lax.broadcasted_iota(jnp.int32, (tokens, tokens), 1)
    same = jnp.where(down == along, 1.0, 0.0).astype(BF)
    before = jnp.where(along < down, 1.0, 0.0).astype(BF)

    def turn(matrix, value):
        return lax.dot_general(
            matrix, value, (((1,), (1,)), ((), ())), preferred_element_type=F32
        )

    return turn(same, gate.astype(BF)), turn(before, mark.astype(BF))


def put_gates(out_ref, at, lanes, columns, picks, lane_slot):
    gate, slot = columns

    def chosen(value):
        result = value[:, picks[-1] : picks[-1] + 1]
        for lane, pick in reversed(list(zip(lanes, picks[:-1], strict=True))):
            result = jnp.where(lane, value[:, pick : pick + 1], result)
        return result

    here = chosen(slot) == lane_slot
    out_ref[at] = jnp.where(here, chosen(gate), 0.0).astype(BF)


def own_lanes(pair, goal):
    lane = lax.broadcasted_iota(jnp.int32, (1, pair), 1)
    first = lane < pair // NC
    inner = jnp.where(first, lane, lane - pair // NC)
    return first, jnp.where(inner % NZ == goal, inner // NZ, -1).astype(F32)


def position(me):
    return me // (NY * NC), (me // NC) % NY, me % NC


def column_kernel(order, me_ref, info_ref, out_ref):
    sources, _, pair = out_ref.shape
    tokens = info_ref.shape[2]
    z, y, c = position(me_ref[0])
    experts = [
        device_at(z, (y + NY - behind) % NY, (c + core) % NC)
        for behind in ROWS_FROM
        for core in range(NC)
    ]
    for number, place in enumerate(order):
        columns = turned(info_ref[(z + place) % NZ], experts)
        first, lane_slot = own_lanes(pair, (z + place) % NZ)
        for source in range(sources):
            picks = (NC * source, NC * source + 1)
            at = (source, slice(number * tokens, (number + 1) * tokens), slice(None))
            put_gates(out_ref, at, [first], columns, picks, lane_slot)


def column_matrix(me, info, order, capacity):
    tokens = info.shape[2]
    sources, pair = len(ROWS_FROM), NC * capacity * NZ
    return pl.pallas_call(
        functools.partial(column_kernel, order),
        grid_spec=pltpu.PrefetchScalarGridSpec(
            num_scalar_prefetch=1,
            grid=(1,),
            in_specs=[pl.BlockSpec(info.shape, lambda i, p: (0, 0, 0))],
            out_specs=pl.BlockSpec((sources, len(order) * tokens, pair), lambda i, p: (0, 0, 0)),
        ),
        out_shape=jax.ShapeDtypeStruct((sources, len(order) * tokens, pair), BF),
        compiler_params=pltpu.CompilerParams(vmem_limit_bytes=VMEM),
        cost_estimate=QUICK,
        name="gatescolumn",
    )(me.reshape(1), info)


def pack_kernel(kept_ref, other_ref, *out_refs):
    block = out_refs[0].shape[0] // NC
    for part, ref in enumerate(out_refs):
        ref[:block] = kept_ref[part * block : (part + 1) * block]
        ref[block:] = other_ref[part * block : (part + 1) * block]


def pack(kept, other, start, columns):
    size = kept.shape[0]
    tile, pair = 512, NC * size // NY
    cost = pl.CostEstimate(flops=0, bytes_accessed=8 * size * columns, transcendentals=0)
    return pl.pallas_call(
        pack_kernel,
        grid=(columns // tile,),
        in_specs=[pl.BlockSpec((size, tile), lambda i: (0, start // tile + i))] * 2,
        out_specs=[pl.BlockSpec((pair, tile), lambda i: (0, i))] * NY,
        out_shape=[jax.ShapeDtypeStruct((pair, columns), BF)] * NY,
        compiler_params=pltpu.CompilerParams(vmem_limit_bytes=LARGE),
        cost_estimate=cost,
        name="pack",
    )(kept, other)


def merge_kernel(matrix_ref, *refs):
    rows, out_ref = refs[:-1], refs[-1]
    total = None
    for part, ref in enumerate(rows):
        term = jnp.dot(matrix_ref[part], ref[...], preferred_element_type=F32)
        total = term if total is None else total + term
    out_ref[...] = total.astype(out_ref.dtype)


def merge_rows(matrix, rows, dtype):
    sources, places, depth = matrix.shape
    columns = rows[0].shape[1]
    tile = 256 if columns % 256 == 0 else 128
    return pl.pallas_call(
        merge_kernel,
        grid=(columns // tile,),
        in_specs=[pl.BlockSpec((sources, places, depth), lambda i: (0, 0, 0))]
        + [pl.BlockSpec((depth, tile), lambda i: (0, i))] * sources,
        out_specs=pl.BlockSpec((places, tile), lambda i: (0, i)),
        out_shape=jax.ShapeDtypeStruct((places, columns), dtype),
        compiler_params=pltpu.CompilerParams(vmem_limit_bytes=VMEM),
        cost_estimate=QUICK,
        name="merge",
    )(matrix, *rows)


def ring_kernel(moves, given, *refs):
    ins, outs = refs[:given], refs[given:]
    for out, at, pieces in moves:
        first, start, rows, _ = pieces[0]
        value = ins[first][start : start + rows].astype(F32)
        for source, begin, count, offset in pieces[1:]:
            more = ins[source][begin : begin + count].astype(F32)
            if count < rows:
                sides = [value[:offset], value[offset + count :]]
                sides = [[jnp.zeros_like(side)] if side.shape[0] else [] for side in sides]
                more = jnp.concatenate([*sides[0], more, *sides[1]], axis=0)
            value = value + more
        outs[out][at : at + rows] = value.astype(BF)


def ring_step(inputs, moves, out_rows):
    columns = inputs[0][0].shape[1]
    tile = columns // 2
    return pl.pallas_call(
        functools.partial(ring_kernel, moves, len(inputs)),
        grid=(2,),
        in_specs=[
            pl.BlockSpec((rows, tile), functools.partial(lambda block, i: (block, i), block))
            for _, rows, block in inputs
        ],
        out_specs=[pl.BlockSpec((rows, tile), lambda i: (0, i)) for rows in out_rows],
        out_shape=[jax.ShapeDtypeStruct((rows, columns), BF) for rows in out_rows],
        compiler_params=pltpu.CompilerParams(vmem_limit_bytes=VMEM),
        cost_estimate=QUICK,
        name="ringstep",
    )(*[value for value, _, _ in inputs])


def last_kernel(done_ref, part_ref, ahead_ref, back_ref, out_ref):
    early = pl.program_id(0) < pl.num_programs(0) // 2

    @pl.when(early)
    def _():
        out_ref[...] = done_ref[...]

    @pl.when(jnp.logical_not(early))
    def _():
        total = part_ref[...] + ahead_ref[...].astype(F32) + back_ref[...].astype(F32)
        out_ref[...] = total.astype(BF)


def whole(value):
    return (value, value.shape[0], 0)


def rings(first, second, tokens, hold):
    half = tokens // 2

    def part(rest, apart):
        return (rest, tokens, ORDER.index(apart))

    def both(step, ahead, back):
        ahead, back = hold(step, [ahead, back])
        with jax.named_scope(f"step{step}"):
            return shift(ahead, dz=1), shift(back, dz=-1)

    def plain(rest, apart, ahead, back):
        return ring_step(
            [part(rest, apart), part(rest, NZ - apart), whole(ahead), whole(back)],
            [
                (0, 0, [(0, 0, tokens, 0), (2, 0, tokens, 0)]),
                (1, 0, [(1, 0, tokens, 0), (3, 0, tokens, 0)]),
            ],
            [tokens] * 2,
        )

    ahead, back = ring_step(
        [part(first, 4)], [(0, 0, [(0, 0, half, 0)]), (1, 0, [(0, half, half, 0)])], [half] * 2
    )
    ahead, back = both(1, ahead, back)
    ahead, back = ring_step(
        [part(first, 3), part(first, 5), whole(ahead), whole(back)],
        [
            (0, 0, [(0, 0, tokens, 0), (2, 0, half, 0)]),
            (1, 0, [(1, 0, tokens, 0), (3, 0, half, half)]),
        ],
        [tokens] * 2,
    )
    ahead, back = both(2, ahead, back)
    ahead, back = both(3, *plain(first, 2, ahead, back))
    later = second()
    ahead, back = ring_step(
        [part(first, 1), part(first, 7), part(later, 4), whole(ahead), whole(back)],
        [
            (0, 0, [(0, 0, tokens, 0), (3, 0, tokens, 0)]),
            (0, tokens, [(2, 0, half, 0)]),
            (1, 0, [(1, 0, tokens, 0), (4, 0, tokens, 0)]),
            (1, tokens, [(2, half, half, 0)]),
        ],
        [tokens + half] * 2,
    )
    ahead, back = both(4, ahead, back)
    done, ahead, back = ring_step(
        [part(first, 0), part(later, 3), part(later, 5), whole(ahead), whole(back)],
        [
            (1, 0, [(1, 0, tokens, 0), (3, tokens, half, 0)]),
            (2, 0, [(2, 0, tokens, 0), (4, tokens, half, half)]),
            (0, 0, [(0, 0, tokens, 0), (3, 0, tokens, 0), (4, 0, tokens, 0)]),
        ],
        [tokens] * 3,
    )
    ahead, back = both(5, ahead, back)
    ahead, back = both(6, *plain(later, 2, ahead, back))
    ahead, back = both(7, *plain(later, 1, ahead, back))
    columns = done.shape[1]
    tile, tiles = columns // 2, 2
    later_tile = lambda i: jnp.maximum(i - tiles, 0)
    return pl.pallas_call(
        last_kernel,
        grid=(2 * tiles,),
        in_specs=[
            pl.BlockSpec((tokens, tile), lambda i: (0, jnp.minimum(i, tiles - 1))),
            pl.BlockSpec((tokens, tile), lambda i: (ORDER.index(0), later_tile(i))),
        ]
        + [pl.BlockSpec((tokens, tile), lambda i: (0, later_tile(i)))] * 2,
        out_specs=pl.BlockSpec((tokens, tile), lambda i: (0, i)),
        out_shape=jax.ShapeDtypeStruct((tokens, 2 * columns), BF),
        compiler_params=pltpu.CompilerParams(vmem_limit_bytes=VMEM),
        cost_estimate=QUICK,
        name="last",
    )(done, later, ahead, back)


ROWS_FROM = (0, 1, 3, 2)
ORDER = (4, 3, 5, 2, 6, 1, 7, 0)
BEHIND = (0, -1, 1, -2, 2)


def holds(input_grad, taps_at):
    moved = {step: [taps_at[step - 1]] for step in (4, 5, 6, 7)}
    return {2: [taps_at[1]], 3: [taps_at[2], input_grad]} | moved


def expert_part(
    routes,
    combine_weights,
    expert_rows,
    expert_weight,
    conv_grad,
    conv_input,
    conv_weight,
    tokens_total,
):
    me = lax.axis_index("expert")
    z, y, c = me // (NY * NC), (me // NC) % NY, me % NC
    capacity = expert_rows.shape[3]
    tokens, top = routes.shape
    block = capacity * NZ
    half = NY * block

    with jax.named_scope("sort"):
        rows = jnp.transpose(expert_rows[0, 0], (1, 0, 2))
        rows = sort_rows(rows, y, c)

    starts = [sum(WIDTHS[:chunk]) for chunk in range(len(WIDTHS))]

    with jax.named_scope("multiply"):
        out = jnp.dot(rows[half:], expert_weight[0], preferred_element_type=F32).astype(BF)
        kept = after(rows, out)[:half]
        kept = jnp.dot(kept, expert_weight[0], preferred_element_type=F32).astype(BF)
    with jax.named_scope("swap"):
        other = shift(out, dc=1)

    def ready(chunk, *first):
        with jax.named_scope(f"pack{chunk}"):
            return pack(after(kept, *first), other, starts[chunk], WIDTHS[chunk])

    def exchange(chunk, parts):
        with jax.named_scope(f"rows{chunk}"):
            return [parts[0]] + [shift(parts[apart], dy=apart) for apart in ROWS_FROM[1:]]

    count = len(WIDTHS)
    edges = conv_edges(after(conv_grad, rows), after(conv_input, rows))
    parts = [ready(0, *edges)]
    parts.append(ready(1, *parts[0][1:]))
    arrived = [exchange(0, parts[0])]
    begin = parts[0][1:]
    with jax.named_scope("info"):
        own = jnp.concatenate([routes.T.astype(F32), combine_weights.T], axis=0)[None]
        column = after(jnp.broadcast_to(own, (NZ, *own.shape[1:])), *begin, *parts[1][1:])
        groups = [
            [device_at(place, row, core) for place in range(NZ)]
            for row in range(NY)
            for core in range(NC)
        ]
        column = lax.all_to_all(
            column, "expert", split_axis=0, concat_axis=0, tiled=True, axis_index_groups=groups
        )
    with jax.named_scope("gatescolumn"):
        matrix = column_matrix(me, column, ORDER, capacity)
    kernel = conv_taps(after(conv_weight, *begin))
    result, taps = conv_local(
        after(conv_grad, *begin), after(conv_input, *begin), edges, kernel
    )
    taps = taps_move(taps) * (1.0 / math.sqrt(tokens_total))
    waited = [*arrived[0][1:], matrix, taps]
    arrived.append(exchange(1, [after(part, *waited) for part in parts[1]]))
    input_grad = conv_move(result)

    taps_at = [taps]
    for number, partner in enumerate(PARTNERS):
        with jax.named_scope(f"taps{number}"):
            taps_at.append(flip_sum(taps_at[-1], partner))

    first = merge_rows(matrix, [after(value, *parts[1][1:]) for value in arrived[0]], F32)

    def second():
        return merge_rows(matrix, arrived[1], F32)

    before = holds(input_grad, taps_at)

    def hold(step, values):
        return [after(value, *before[step]) for value in values] if step in before else values

    token_grad = rings(first, second, tokens, hold)
    return token_grad, input_grad, taps_at[-1]


def local(routes, combine_weights, expert_rows, expert_weight, conv_grad, conv_input, conv_weight):
    tokens_total = routes.shape[0] * lax.axis_size("expert") * lax.axis_size("seq")
    return expert_part(
        routes,
        combine_weights,
        expert_rows,
        expert_weight,
        conv_grad,
        conv_input,
        conv_weight,
        tokens_total,
    )


def solution(mesh):
    placed = (
        P(("expert", "seq"), None),
        P(("expert", "seq"), None),
        P("expert", "seq", None, None, None),
        P("expert", None, None),
        P(("expert", "seq"), None),
        P(("expert", "seq"), None),
        P(None, "seq"),
    )
    return jax.shard_map(
        local,
        mesh=mesh,
        in_specs=placed,
        out_specs=(P(("expert", "seq"), None), P("expert", "seq"), P(None, "seq")),
        check_vma=False,
    )
```

```python
import functools
import math

import jax
import jax.numpy as jnp
from jax import lax
from jax.experimental import pallas as pl
from jax.experimental.pallas import tpu as pltpu
from jax.sharding import PartitionSpec as P

NZ, NY, NC = 8, 4, 2
REACH = 3
WIDTHS = (1024, 1024)
BF = jnp.bfloat16
F32 = jnp.float32
VMEM = 40 * 1024 * 1024
LARGE = 58 * 1024 * 1024
FILLS = pl.CostEstimate(flops=0, bytes_accessed=12_000_000, transcendentals=0)
QUICK = pl.CostEstimate(flops=0, bytes_accessed=0, transcendentals=0)


def device_at(z, y, c):
    return (z * NY + y) * NC + c


def shift(value, dz=0, dy=0, dc=0):
    pairs = [
        (device_at(z, y, c), device_at((z + dz) % NZ, (y + dy) % NY, (c + dc) % NC))
        for z in range(NZ)
        for y in range(NY)
        for c in range(NC)
    ]
    return lax.ppermute(value, "expert", pairs)


def after(value, *first):
    return lax.optimization_barrier((value, *first))[0]


def from_behind(value, axis, steps):
    count = lax.axis_size(axis)
    leading, last = (max(0, -steps), min(count, count - steps))
    return lax.ppermute(value, axis, [(source, source + steps) for source in range(leading, last)])


def conv_kernel(grad_ref, input_ref, taps_ref, result_ref, sums_ref):
    count, reach = result_ref.shape[0], taps_ref.shape[0] - 1
    inputs = input_ref[...].astype(F32)
    near = [inputs[offset : offset + count + reach] for offset in range(reach + 1)]
    taps = [taps_ref[offset : offset + 1] for offset in range(reach + 1)]
    pre_act = taps[0] * near[0]
    for offset in range(1, reach + 1):
        pre_act = pre_act + taps[offset] * near[offset]
    sigmoid = 1.0 / (1.0 + jnp.exp(-pre_act))
    pre_grad = grad_ref[...].astype(F32) * sigmoid * (1.0 + pre_act * (1.0 - sigmoid))
    result = taps[0] * pre_grad[reach : reach + count]
    for offset in range(1, reach + 1):
        result = result + taps[offset] * pre_grad[reach - offset : reach - offset + count]
    result_ref[...] = result.astype(BF)
    here = pre_grad[:count]
    sums = [jnp.sum(here * near[o][:count], axis=0, keepdims=True) for o in range(reach + 1)]
    sums_ref[...] = jnp.concatenate(sums, axis=0)


def conv_core(grad_rows, input_rows, input_past, grad_next, input_next, kernel):
    count, channels = grad_rows.shape
    taps = kernel.shape[0]
    tile = 256
    input_ext = jnp.concatenate([input_past, input_rows, input_next], axis=0)
    grad_ext = jnp.concatenate([grad_rows, grad_next], axis=0)
    column = lambda i: (0, i)
    return pl.pallas_call(
        conv_kernel,
        grid=(channels // tile,),
        in_specs=[
            pl.BlockSpec((grad_ext.shape[0], tile), column),
            pl.BlockSpec((input_ext.shape[0], tile), column),
            pl.BlockSpec((taps, tile), column),
        ],
        out_specs=[pl.BlockSpec((count, tile), column), pl.BlockSpec((taps, tile), column)],
        out_shape=[
            jax.ShapeDtypeStruct((count, channels), BF),
            jax.ShapeDtypeStruct((taps, channels), F32),
        ],
        compiler_params=pltpu.CompilerParams(vmem_limit_bytes=VMEM),
        cost_estimate=FILLS,
        name="conv",
    )(grad_ext, input_ext, kernel)


def conv_edges(conv_grad, conv_input):
    with jax.named_scope("convedges"):
        past = from_behind(conv_input[-REACH:], ("expert", "seq"), 1)
        front = jnp.stack([conv_grad[:REACH], conv_input[:REACH]], axis=0)
        return past, from_behind(front, ("expert", "seq"), -1)


def conv_taps(conv_weight):
    count = lax.axis_size("seq")
    with jax.named_scope("convtaps"):
        kernel = jnp.broadcast_to(conv_weight[None], (count, *conv_weight.shape))
        kernel = lax.all_to_all(kernel, "seq", split_axis=0, concat_axis=0, tiled=True)
        return jnp.concatenate([kernel[i] for i in range(count)], axis=1)


def conv_local(conv_grad, conv_input, edges, kernel):
    past, front = edges
    with jax.named_scope("convcore"):
        result, taps = conv_core(conv_grad, conv_input, past, front[0], front[1], kernel)
    return result, taps


def taps_move(taps):
    count = lax.axis_size("seq")
    with jax.named_scope("tapsmove"):
        width = taps.shape[1] // count
        taps = jnp.stack([taps[:, i * width : (i + 1) * width] for i in range(count)])
        taps = lax.all_to_all(taps, "seq", split_axis=0, concat_axis=0, tiled=True)
        return jnp.sum(taps, axis=0)


def keep_kernel(value_ref, out_ref):
    out_ref[...] = value_ref[...]


def conv_move(result):
    with jax.named_scope("convmove"):
        result = lax.all_to_all(result, "seq", split_axis=1, concat_axis=0, tiled=True)
        rows, columns = result.shape
        block = pl.BlockSpec((rows // 4, columns), lambda i: (i, 0))
        return pl.pallas_call(
            keep_kernel,
            grid=(4,),
            in_specs=[block],
            out_specs=block,
            out_shape=jax.ShapeDtypeStruct(result.shape, BF),
            cost_estimate=QUICK,
            name="keep",
        )(result)


PARTNERS = (
    lambda z, y, c: (z, y, c ^ 1),
    lambda z, y, c: (z ^ 4, y, c),
    lambda z, y, c: (z ^ 2, y, c),
    lambda z, y, c: (z ^ 1, y, c),
    lambda z, y, c: (z, y ^ 1, c),
    lambda z, y, c: (z, y ^ 2, c),
)


def flip_sum(value, partner):
    pairs = [
        (device_at(z, y, c), device_at(*partner(z, y, c)))
        for z in range(NZ)
        for y in range(NY)
        for c in range(NC)
    ]
    return value + lax.ppermute(value, "expert", pairs)


def sort_kernel(order_ref, rows_ref, out_ref):
    order = order_ref[...]
    parts = out_ref.shape[0]
    for group in range(rows_ref.shape[0]):
        moved = jnp.dot(order, rows_ref[group], preferred_element_type=F32).astype(BF)
        out_ref[:, group] = moved.reshape(parts, moved.shape[0] // parts, moved.shape[1])


def sort_rows(rows, y, c):
    capacity, groups, depth = rows.shape
    parts = NY * NC
    size = 2 * groups
    count = capacity // 2
    rows = rows.reshape(count, size, depth)
    place = lax.broadcasted_iota(jnp.int32, (size, size), 0)
    source = lax.broadcasted_iota(jnp.int32, (size, size), 1)
    part, inner = place // (2 * NZ), place % (2 * NZ)
    core, row = (c + part // NY) % NC, (y + part % NY) % NY
    wanted = (inner // NZ) * groups + (inner % NZ) * parts + row * NC + core
    order = (source == wanted).astype(BF)
    step = 5 if count % 5 == 0 else 1
    out = pl.pallas_call(
        sort_kernel,
        grid=(count // step,),
        in_specs=[
            pl.BlockSpec((size, size), lambda i: (0, 0)),
            pl.BlockSpec((step, size, depth), lambda i: (i, 0, 0)),
        ],
        out_specs=pl.BlockSpec((parts, step, size // parts, depth), lambda i: (0, i, 0, 0)),
        out_shape=jax.ShapeDtypeStruct((parts, count, size // parts, depth), BF),
        compiler_params=pltpu.CompilerParams(vmem_limit_bytes=VMEM),
        cost_estimate=QUICK,
        name="sort",
    )(order, rows)
    return out.reshape(parts * count * (size // parts), depth)


def turned(info, experts):
    top, tokens = info.shape[0] // 2, info.shape[1]
    named, gates = info[:top], info[top:]
    rows, marks = [], []
    for expert in experts:
        hit = named == expert.astype(F32)
        rows.append(jnp.sum(jnp.where(hit, gates, 0.0), axis=0, keepdims=True))
        marks.append(jnp.sum(jnp.where(hit, 1.0, 0.0), axis=0, keepdims=True))
    gate, mark = jnp.concatenate(rows, axis=0), jnp.concatenate(marks, axis=0)
    down = lax.broadcasted_iota(jnp.int32, (tokens, tokens), 0)
    along = lax.broadcasted_iota(jnp.int32, (tokens, tokens), 1)
    same = jnp.where(down == along, 1.0, 0.0).astype(BF)
    before = jnp.where(along < down, 1.0, 0.0).astype(BF)

    def turn(matrix, value):
        return lax.dot_general(
            matrix, value, (((1,), (1,)), ((), ())), preferred_element_type=F32
        )

    return turn(same, gate.astype(BF)), turn(before, mark.astype(BF))


def put_gates(out_ref, at, lanes, columns, picks, lane_slot):
    gate, slot = columns

    def chosen(value):
        result = value[:, picks[-1] : picks[-1] + 1]
        for lane, pick in reversed(list(zip(lanes, picks[:-1], strict=True))):
            result = jnp.where(lane, value[:, pick : pick + 1], result)
        return result

    here = chosen(slot) == lane_slot
    out_ref[at] = jnp.where(here, chosen(gate), 0.0).astype(BF)


def own_lanes(pair, goal):
    lane = lax.broadcasted_iota(jnp.int32, (1, pair), 1)
    first = lane < pair // NC
    inner = jnp.where(first, lane, lane - pair // NC)
    return first, jnp.where(inner % NZ == goal, inner // NZ, -1).astype(F32)


def position(me):
    return me // (NY * NC), (me // NC) % NY, me % NC


def column_kernel(order, me_ref, info_ref, out_ref):
    sources, _, pair = out_ref.shape
    tokens = info_ref.shape[2]
    z, y, c = position(me_ref[0])
    experts = [
        device_at(z, (y + NY - behind) % NY, (c + core) % NC)
        for behind in ROWS_FROM
        for core in range(NC)
    ]
    for number, place in enumerate(order):
        columns = turned(info_ref[(z + place) % NZ], experts)
        first, lane_slot = own_lanes(pair, (z + place) % NZ)
        for source in range(sources):
            picks = (NC * source, NC * source + 1)
            at = (source, slice(number * tokens, (number + 1) * tokens), slice(None))
            put_gates(out_ref, at, [first], columns, picks, lane_slot)


def column_matrix(me, info, order, capacity):
    tokens = info.shape[2]
    sources, pair = len(ROWS_FROM), NC * capacity * NZ
    return pl.pallas_call(
        functools.partial(column_kernel, order),
        grid_spec=pltpu.PrefetchScalarGridSpec(
            num_scalar_prefetch=1,
            grid=(1,),
            in_specs=[pl.BlockSpec(info.shape, lambda i, p: (0, 0, 0))],
            out_specs=pl.BlockSpec((sources, len(order) * tokens, pair), lambda i, p: (0, 0, 0)),
        ),
        out_shape=jax.ShapeDtypeStruct((sources, len(order) * tokens, pair), BF),
        compiler_params=pltpu.CompilerParams(vmem_limit_bytes=VMEM),
        cost_estimate=FILLS,
        name="gatescolumn",
    )(me.reshape(1), info)


def pack_kernel(kept_ref, other_ref, *out_refs):
    block = out_refs[0].shape[0] // NC
    for part, ref in enumerate(out_refs):
        ref[:block] = kept_ref[part * block : (part + 1) * block]
        ref[block:] = other_ref[part * block : (part + 1) * block]


def pack(kept, other, start, columns):
    size = kept.shape[0]
    tile, pair = 512, NC * size // NY
    cost = pl.CostEstimate(flops=0, bytes_accessed=8 * size * columns, transcendentals=0)
    return pl.pallas_call(
        pack_kernel,
        grid=(columns // tile,),
        in_specs=[pl.BlockSpec((size, tile), lambda i: (0, start // tile + i))] * 2,
        out_specs=[pl.BlockSpec((pair, tile), lambda i: (0, i))] * NY,
        out_shape=[jax.ShapeDtypeStruct((pair, columns), BF)] * NY,
        compiler_params=pltpu.CompilerParams(vmem_limit_bytes=LARGE),
        cost_estimate=cost,
        name="pack",
    )(kept, other)


def merge_kernel(matrix_ref, *refs):
    rows, out_ref = refs[:-1], refs[-1]
    total = None
    for part, ref in enumerate(rows):
        term = jnp.dot(matrix_ref[part], ref[...], preferred_element_type=F32)
        total = term if total is None else total + term
    out_ref[...] = total.astype(out_ref.dtype)


def merge_rows(matrix, rows, dtype):
    sources, places, depth = matrix.shape
    columns = rows[0].shape[1]
    tile = 256 if columns % 256 == 0 else 128
    return pl.pallas_call(
        merge_kernel,
        grid=(columns // tile,),
        in_specs=[pl.BlockSpec((sources, places, depth), lambda i: (0, 0, 0))]
        + [pl.BlockSpec((depth, tile), lambda i: (0, i))] * sources,
        out_specs=pl.BlockSpec((places, tile), lambda i: (0, i)),
        out_shape=jax.ShapeDtypeStruct((places, columns), dtype),
        compiler_params=pltpu.CompilerParams(vmem_limit_bytes=VMEM),
        cost_estimate=QUICK,
        name="merge",
    )(matrix, *rows)


def ring_kernel(moves, given, *refs):
    ins, outs = refs[:given], refs[given:]
    for out, at, pieces in moves:
        first, start, rows, _ = pieces[0]
        value = ins[first][start : start + rows].astype(F32)
        for source, begin, count, offset in pieces[1:]:
            more = ins[source][begin : begin + count].astype(F32)
            if count < rows:
                sides = [value[:offset], value[offset + count :]]
                sides = [[jnp.zeros_like(side)] if side.shape[0] else [] for side in sides]
                more = jnp.concatenate([*sides[0], more, *sides[1]], axis=0)
            value = value + more
        outs[out][at : at + rows] = value.astype(BF)


def ring_step(inputs, moves, out_rows):
    columns = inputs[0][0].shape[1]
    tile = columns // 2
    return pl.pallas_call(
        functools.partial(ring_kernel, moves, len(inputs)),
        grid=(2,),
        in_specs=[
            pl.BlockSpec((rows, tile), functools.partial(lambda block, i: (block, i), block))
            for _, rows, block in inputs
        ],
        out_specs=[pl.BlockSpec((rows, tile), lambda i: (0, i)) for rows in out_rows],
        out_shape=[jax.ShapeDtypeStruct((rows, columns), BF) for rows in out_rows],
        compiler_params=pltpu.CompilerParams(vmem_limit_bytes=VMEM),
        cost_estimate=QUICK,
        name="ringstep",
    )(*[value for value, _, _ in inputs])


def last_kernel(done_ref, part_ref, ahead_ref, back_ref, out_ref):
    early = pl.program_id(0) < pl.num_programs(0) // 2

    @pl.when(early)
    def _():
        out_ref[...] = done_ref[...]

    @pl.when(jnp.logical_not(early))
    def _():
        total = part_ref[...] + ahead_ref[...].astype(F32) + back_ref[...].astype(F32)
        out_ref[...] = total.astype(BF)


def whole(value):
    return (value, value.shape[0], 0)


def rings(first, second, tokens, hold):
    half = tokens // 2

    def part(rest, apart):
        return (rest, tokens, ORDER.index(apart))

    def both(step, ahead, back):
        ahead, back = hold(step, [ahead, back])
        with jax.named_scope(f"step{step}"):
            return shift(ahead, dz=1), shift(back, dz=-1)

    def plain(rest, apart, ahead, back):
        return ring_step(
            [part(rest, apart), part(rest, NZ - apart), whole(ahead), whole(back)],
            [
                (0, 0, [(0, 0, tokens, 0), (2, 0, tokens, 0)]),
                (1, 0, [(1, 0, tokens, 0), (3, 0, tokens, 0)]),
            ],
            [tokens] * 2,
        )

    ahead, back = ring_step(
        [part(first, 4)], [(0, 0, [(0, 0, half, 0)]), (1, 0, [(0, half, half, 0)])], [half] * 2
    )
    ahead, back = both(1, ahead, back)
    ahead, back = ring_step(
        [part(first, 3), part(first, 5), whole(ahead), whole(back)],
        [
            (0, 0, [(0, 0, tokens, 0), (2, 0, half, 0)]),
            (1, 0, [(1, 0, tokens, 0), (3, 0, half, half)]),
        ],
        [tokens] * 2,
    )
    ahead, back = both(2, ahead, back)
    ahead, back = both(3, *plain(first, 2, ahead, back))
    later = second()
    ahead, back = ring_step(
        [part(first, 1), part(first, 7), part(later, 4), whole(ahead), whole(back)],
        [
            (0, 0, [(0, 0, tokens, 0), (3, 0, tokens, 0)]),
            (0, tokens, [(2, 0, half, 0)]),
            (1, 0, [(1, 0, tokens, 0), (4, 0, tokens, 0)]),
            (1, tokens, [(2, half, half, 0)]),
        ],
        [tokens + half] * 2,
    )
    ahead, back = both(4, ahead, back)
    done, ahead, back = ring_step(
        [part(first, 0), part(later, 3), part(later, 5), whole(ahead), whole(back)],
        [
            (1, 0, [(1, 0, tokens, 0), (3, tokens, half, 0)]),
            (2, 0, [(2, 0, tokens, 0), (4, tokens, half, half)]),
            (0, 0, [(0, 0, tokens, 0), (3, 0, tokens, 0), (4, 0, tokens, 0)]),
        ],
        [tokens] * 3,
    )
    ahead, back = both(5, ahead, back)
    ahead, back = both(6, *plain(later, 2, ahead, back))
    ahead, back = both(7, *plain(later, 1, ahead, back))
    columns = done.shape[1]
    tile, tiles = columns // 2, 2
    later_tile = lambda i: jnp.maximum(i - tiles, 0)
    return pl.pallas_call(
        last_kernel,
        grid=(2 * tiles,),
        in_specs=[
            pl.BlockSpec((tokens, tile), lambda i: (0, jnp.minimum(i, tiles - 1))),
            pl.BlockSpec((tokens, tile), lambda i: (ORDER.index(0), later_tile(i))),
        ]
        + [pl.BlockSpec((tokens, tile), lambda i: (0, later_tile(i)))] * 2,
        out_specs=pl.BlockSpec((tokens, tile), lambda i: (0, i)),
        out_shape=jax.ShapeDtypeStruct((tokens, 2 * columns), BF),
        compiler_params=pltpu.CompilerParams(vmem_limit_bytes=VMEM),
        cost_estimate=QUICK,
        name="last",
    )(done, later, ahead, back)


ROWS_FROM = (0, 1, 3, 2)
ORDER = (4, 3, 5, 2, 6, 1, 7, 0)
BEHIND = (0, -1, 1, -2, 2)


def holds(input_grad, taps_at):
    moved = {step: [taps_at[step - 1]] for step in (4, 5, 6, 7)}
    return {2: [taps_at[1]], 3: [taps_at[2], input_grad]} | moved


def expert_part(
    routes,
    combine_weights,
    expert_rows,
    expert_weight,
    conv_grad,
    conv_input,
    conv_weight,
    tokens_total,
):
    me = lax.axis_index("expert")
    z, y, c = me // (NY * NC), (me // NC) % NY, me % NC
    capacity = expert_rows.shape[3]
    tokens, top = routes.shape
    block = capacity * NZ
    half = NY * block

    with jax.named_scope("sort"):
        rows = jnp.transpose(expert_rows[0, 0], (1, 0, 2))
        rows = sort_rows(rows, y, c)

    starts = [sum(WIDTHS[:chunk]) for chunk in range(len(WIDTHS))]

    with jax.named_scope("multiply"):
        out = jnp.dot(rows[half:], expert_weight[0], preferred_element_type=F32).astype(BF)
        kept = after(rows, out)[:half]
        kept = jnp.dot(kept, expert_weight[0], preferred_element_type=F32).astype(BF)
    with jax.named_scope("swap"):
        other = shift(out, dc=1)

    def ready(chunk, *first):
        with jax.named_scope(f"pack{chunk}"):
            return pack(after(kept, *first), other, starts[chunk], WIDTHS[chunk])

    def exchange(chunk, parts):
        with jax.named_scope(f"rows{chunk}"):
            return [parts[0]] + [shift(parts[apart], dy=apart) for apart in ROWS_FROM[1:]]

    count = len(WIDTHS)
    edges = conv_edges(after(conv_grad, rows), after(conv_input, rows))
    parts = [ready(0, *edges)]
    parts.append(ready(1, *parts[0][1:]))
    arrived = [exchange(0, parts[0])]
    begin = parts[0][1:]
    with jax.named_scope("info"):
        own = jnp.concatenate([routes.T.astype(F32), combine_weights.T], axis=0)[None]
        column = after(jnp.broadcast_to(own, (NZ, *own.shape[1:])), *begin)
        groups = [
            [device_at(place, row, core) for place in range(NZ)]
            for row in range(NY)
            for core in range(NC)
        ]
        column = lax.all_to_all(
            column, "expert", split_axis=0, concat_axis=0, tiled=True, axis_index_groups=groups
        )
    with jax.named_scope("gatescolumn"):
        matrix = column_matrix(me, column, ORDER, capacity)
    kernel = conv_taps(after(conv_weight, *begin))
    result, taps = conv_local(
        after(conv_grad, *begin), after(conv_input, *begin), edges, kernel
    )
    taps = taps_move(after(taps, column)) * (1.0 / math.sqrt(tokens_total))
    input_grad = conv_move(result)
    waited = [*arrived[0][1:], matrix, taps]
    arrived.append(exchange(1, [after(part, *waited) for part in parts[1]]))

    taps_at = [taps]
    for number, partner in enumerate(PARTNERS):
        with jax.named_scope(f"taps{number}"):
            taps_at.append(flip_sum(taps_at[-1], partner))

    first = merge_rows(matrix, [after(value, *parts[1][1:]) for value in arrived[0]], F32)

    def second():
        return merge_rows(matrix, arrived[1], F32)

    before = holds(input_grad, taps_at)

    def hold(step, values):
        return [after(value, *before[step]) for value in values] if step in before else values

    token_grad = rings(first, second, tokens, hold)
    return token_grad, input_grad, taps_at[-1]


def local(routes, combine_weights, expert_rows, expert_weight, conv_grad, conv_input, conv_weight):
    tokens_total = routes.shape[0] * lax.axis_size("expert") * lax.axis_size("seq")
    return expert_part(
        routes,
        combine_weights,
        expert_rows,
        expert_weight,
        conv_grad,
        conv_input,
        conv_weight,
        tokens_total,
    )


def solution(mesh):
    placed = (
        P(("expert", "seq"), None),
        P(("expert", "seq"), None),
        P("expert", "seq", None, None, None),
        P("expert", None, None),
        P(("expert", "seq"), None),
        P(("expert", "seq"), None),
        P(None, "seq"),
    )
    return jax.shard_map(
        local,
        mesh=mesh,
        in_specs=placed,
        out_specs=(P(("expert", "seq"), None), P("expert", "seq"), P(None, "seq")),
        check_vma=False,
    )
```

```python
import functools
import math

import jax
import jax.numpy as jnp
from jax import lax
from jax.experimental import pallas as pl
from jax.experimental.pallas import tpu as pltpu
from jax.sharding import PartitionSpec as P

NZ, NY, NC = 8, 4, 2
REACH = 3
WIDTHS = (1024, 1024)
BF = jnp.bfloat16
F32 = jnp.float32
VMEM = 40 * 1024 * 1024
LARGE = 58 * 1024 * 1024
FILLS = pl.CostEstimate(flops=0, bytes_accessed=12_000_000, transcendentals=0)
QUICK = pl.CostEstimate(flops=0, bytes_accessed=0, transcendentals=0)


def device_at(z, y, c):
    return (z * NY + y) * NC + c


def shift(value, dz=0, dy=0, dc=0):
    pairs = [
        (device_at(z, y, c), device_at((z + dz) % NZ, (y + dy) % NY, (c + dc) % NC))
        for z in range(NZ)
        for y in range(NY)
        for c in range(NC)
    ]
    return lax.ppermute(value, "expert", pairs)


def after(value, *first):
    return lax.optimization_barrier((value, *first))[0]


def from_behind(value, axis, steps):
    count = lax.axis_size(axis)
    leading, last = (max(0, -steps), min(count, count - steps))
    return lax.ppermute(value, axis, [(source, source + steps) for source in range(leading, last)])


def conv_kernel(grad_ref, input_ref, taps_ref, result_ref, sums_ref):
    count, reach = result_ref.shape[0], taps_ref.shape[0] - 1
    inputs = input_ref[...].astype(F32)
    near = [inputs[offset : offset + count + reach] for offset in range(reach + 1)]
    taps = [taps_ref[offset : offset + 1] for offset in range(reach + 1)]
    pre_act = taps[0] * near[0]
    for offset in range(1, reach + 1):
        pre_act = pre_act + taps[offset] * near[offset]
    sigmoid = 1.0 / (1.0 + jnp.exp(-pre_act))
    pre_grad = grad_ref[...].astype(F32) * sigmoid * (1.0 + pre_act * (1.0 - sigmoid))
    result = taps[0] * pre_grad[reach : reach + count]
    for offset in range(1, reach + 1):
        result = result + taps[offset] * pre_grad[reach - offset : reach - offset + count]
    result_ref[...] = result.astype(BF)
    here = pre_grad[:count]
    sums = [jnp.sum(here * near[o][:count], axis=0, keepdims=True) for o in range(reach + 1)]
    sums_ref[...] = jnp.concatenate(sums, axis=0)


def conv_core(grad_rows, input_rows, input_past, grad_next, input_next, kernel):
    count, channels = grad_rows.shape
    taps = kernel.shape[0]
    tile = 256
    input_ext = jnp.concatenate([input_past, input_rows, input_next], axis=0)
    grad_ext = jnp.concatenate([grad_rows, grad_next], axis=0)
    column = lambda i: (0, i)
    return pl.pallas_call(
        conv_kernel,
        grid=(channels // tile,),
        in_specs=[
            pl.BlockSpec((grad_ext.shape[0], tile), column),
            pl.BlockSpec((input_ext.shape[0], tile), column),
            pl.BlockSpec((taps, tile), column),
        ],
        out_specs=[pl.BlockSpec((count, tile), column), pl.BlockSpec((taps, tile), column)],
        out_shape=[
            jax.ShapeDtypeStruct((count, channels), BF),
            jax.ShapeDtypeStruct((taps, channels), F32),
        ],
        compiler_params=pltpu.CompilerParams(vmem_limit_bytes=VMEM),
        cost_estimate=FILLS,
        name="conv",
    )(grad_ext, input_ext, kernel)


def conv_edges(conv_grad, conv_input):
    with jax.named_scope("convedges"):
        past = from_behind(conv_input[-REACH:], ("expert", "seq"), 1)
        front = jnp.stack([conv_grad[:REACH], conv_input[:REACH]], axis=0)
        return past, from_behind(front, ("expert", "seq"), -1)


def conv_taps(conv_weight):
    count = lax.axis_size("seq")
    with jax.named_scope("convtaps"):
        kernel = jnp.broadcast_to(conv_weight[None], (count, *conv_weight.shape))
        kernel = lax.all_to_all(kernel, "seq", split_axis=0, concat_axis=0, tiled=True)
        return jnp.concatenate([kernel[i] for i in range(count)], axis=1)


def conv_local(conv_grad, conv_input, edges, kernel):
    past, front = edges
    with jax.named_scope("convcore"):
        result, taps = conv_core(conv_grad, conv_input, past, front[0], front[1], kernel)
    return result, taps


def taps_move(taps):
    count = lax.axis_size("seq")
    with jax.named_scope("tapsmove"):
        width = taps.shape[1] // count
        taps = jnp.stack([taps[:, i * width : (i + 1) * width] for i in range(count)])
        taps = lax.all_to_all(taps, "seq", split_axis=0, concat_axis=0, tiled=True)
        return jnp.sum(taps, axis=0)


def keep_kernel(value_ref, out_ref):
    out_ref[...] = value_ref[...]


def conv_move(result):
    with jax.named_scope("convmove"):
        result = lax.all_to_all(result, "seq", split_axis=1, concat_axis=0, tiled=True)
        rows, columns = result.shape
        block = pl.BlockSpec((rows // 4, columns), lambda i: (i, 0))
        return pl.pallas_call(
            keep_kernel,
            grid=(4,),
            in_specs=[block],
            out_specs=block,
            out_shape=jax.ShapeDtypeStruct(result.shape, BF),
            cost_estimate=QUICK,
            name="keep",
        )(result)


PARTNERS = (
    lambda z, y, c: (z, y, c ^ 1),
    lambda z, y, c: (z ^ 4, y, c),
    lambda z, y, c: (z ^ 2, y, c),
    lambda z, y, c: (z ^ 1, y, c),
    lambda z, y, c: (z, y ^ 1, c),
    lambda z, y, c: (z, y ^ 2, c),
)


def flip_sum(value, partner):
    pairs = [
        (device_at(z, y, c), device_at(*partner(z, y, c)))
        for z in range(NZ)
        for y in range(NY)
        for c in range(NC)
    ]
    return value + lax.ppermute(value, "expert", pairs)


def sort_kernel(order_ref, rows_ref, out_ref):
    order = order_ref[...]
    parts = out_ref.shape[0]
    for group in range(rows_ref.shape[0]):
        moved = jnp.dot(order, rows_ref[group], preferred_element_type=F32).astype(BF)
        out_ref[:, group] = moved.reshape(parts, moved.shape[0] // parts, moved.shape[1])


def sort_rows(rows, y, c):
    capacity, groups, depth = rows.shape
    parts = NY * NC
    size = 2 * groups
    count = capacity // 2
    rows = rows.reshape(count, size, depth)
    place = lax.broadcasted_iota(jnp.int32, (size, size), 0)
    source = lax.broadcasted_iota(jnp.int32, (size, size), 1)
    part, inner = place // (2 * NZ), place % (2 * NZ)
    core, row = (c + part // NY) % NC, (y + part % NY) % NY
    wanted = (inner // NZ) * groups + (inner % NZ) * parts + row * NC + core
    order = (source == wanted).astype(BF)
    step = 5 if count % 5 == 0 else 1
    out = pl.pallas_call(
        sort_kernel,
        grid=(count // step,),
        in_specs=[
            pl.BlockSpec((size, size), lambda i: (0, 0)),
            pl.BlockSpec((step, size, depth), lambda i: (i, 0, 0)),
        ],
        out_specs=pl.BlockSpec((parts, step, size // parts, depth), lambda i: (0, i, 0, 0)),
        out_shape=jax.ShapeDtypeStruct((parts, count, size // parts, depth), BF),
        compiler_params=pltpu.CompilerParams(vmem_limit_bytes=VMEM),
        cost_estimate=QUICK,
        name="sort",
    )(order, rows)
    return out.reshape(parts * count * (size // parts), depth)


def turned(info, experts):
    top, tokens = info.shape[0] // 2, info.shape[1]
    named, gates = info[:top], info[top:]
    rows, marks = [], []
    for expert in experts:
        hit = named == expert.astype(F32)
        rows.append(jnp.sum(jnp.where(hit, gates, 0.0), axis=0, keepdims=True))
        marks.append(jnp.sum(jnp.where(hit, 1.0, 0.0), axis=0, keepdims=True))
    gate, mark = jnp.concatenate(rows, axis=0), jnp.concatenate(marks, axis=0)
    down = lax.broadcasted_iota(jnp.int32, (tokens, tokens), 0)
    along = lax.broadcasted_iota(jnp.int32, (tokens, tokens), 1)
    same = jnp.where(down == along, 1.0, 0.0).astype(BF)
    before = jnp.where(along < down, 1.0, 0.0).astype(BF)

    def turn(matrix, value):
        return lax.dot_general(
            matrix, value, (((1,), (1,)), ((), ())), preferred_element_type=F32
        )

    return turn(same, gate.astype(BF)), turn(before, mark.astype(BF))


def put_gates(out_ref, at, lanes, columns, picks, lane_slot):
    gate, slot = columns

    def chosen(value):
        result = value[:, picks[-1] : picks[-1] + 1]
        for lane, pick in reversed(list(zip(lanes, picks[:-1], strict=True))):
            result = jnp.where(lane, value[:, pick : pick + 1], result)
        return result

    here = chosen(slot) == lane_slot
    out_ref[at] = jnp.where(here, chosen(gate), 0.0).astype(BF)


def own_lanes(pair, goal):
    lane = lax.broadcasted_iota(jnp.int32, (1, pair), 1)
    first = lane < pair // NC
    inner = jnp.where(first, lane, lane - pair // NC)
    return first, jnp.where(inner % NZ == goal, inner // NZ, -1).astype(F32)


def position(me):
    return me // (NY * NC), (me // NC) % NY, me % NC


def column_kernel(order, me_ref, info_ref, out_ref):
    sources, _, pair = out_ref.shape
    tokens = info_ref.shape[2]
    z, y, c = position(me_ref[0])
    experts = [
        device_at(z, (y + NY - behind) % NY, (c + core) % NC)
        for behind in ROWS_FROM
        for core in range(NC)
    ]
    for number, place in enumerate(order):
        columns = turned(info_ref[(z + place) % NZ], experts)
        first, lane_slot = own_lanes(pair, (z + place) % NZ)
        for source in range(sources):
            picks = (NC * source, NC * source + 1)
            at = (source, slice(number * tokens, (number + 1) * tokens), slice(None))
            put_gates(out_ref, at, [first], columns, picks, lane_slot)


def column_matrix(me, info, order, capacity):
    tokens = info.shape[2]
    sources, pair = len(ROWS_FROM), NC * capacity * NZ
    return pl.pallas_call(
        functools.partial(column_kernel, order),
        grid_spec=pltpu.PrefetchScalarGridSpec(
            num_scalar_prefetch=1,
            grid=(1,),
            in_specs=[pl.BlockSpec(info.shape, lambda i, p: (0, 0, 0))],
            out_specs=pl.BlockSpec((sources, len(order) * tokens, pair), lambda i, p: (0, 0, 0)),
        ),
        out_shape=jax.ShapeDtypeStruct((sources, len(order) * tokens, pair), BF),
        compiler_params=pltpu.CompilerParams(vmem_limit_bytes=VMEM),
        cost_estimate=FILLS,
        name="gatescolumn",
    )(me.reshape(1), info)


def pack_kernel(kept_ref, other_ref, *out_refs):
    block = out_refs[0].shape[0] // NC
    for part, ref in enumerate(out_refs):
        ref[:block] = kept_ref[part * block : (part + 1) * block]
        ref[block:] = other_ref[part * block : (part + 1) * block]


def pack(kept, other, start, columns):
    size = kept.shape[0]
    tile, pair = 512, NC * size // NY
    cost = pl.CostEstimate(flops=0, bytes_accessed=8 * size * columns, transcendentals=0)
    return pl.pallas_call(
        pack_kernel,
        grid=(columns // tile,),
        in_specs=[pl.BlockSpec((size, tile), lambda i: (0, start // tile + i))] * 2,
        out_specs=[pl.BlockSpec((pair, tile), lambda i: (0, i))] * NY,
        out_shape=[jax.ShapeDtypeStruct((pair, columns), BF)] * NY,
        compiler_params=pltpu.CompilerParams(vmem_limit_bytes=LARGE),
        cost_estimate=cost,
        name="pack",
    )(kept, other)


def merge_kernel(matrix_ref, *refs):
    rows, out_ref = refs[:-1], refs[-1]
    total = None
    for part, ref in enumerate(rows):
        term = jnp.dot(matrix_ref[part], ref[...], preferred_element_type=F32)
        total = term if total is None else total + term
    out_ref[...] = total.astype(out_ref.dtype)


def merge_rows(matrix, rows, dtype):
    sources, places, depth = matrix.shape
    columns = rows[0].shape[1]
    tile = 256 if columns % 256 == 0 else 128
    return pl.pallas_call(
        merge_kernel,
        grid=(columns // tile,),
        in_specs=[pl.BlockSpec((sources, places, depth), lambda i: (0, 0, 0))]
        + [pl.BlockSpec((depth, tile), lambda i: (0, i))] * sources,
        out_specs=pl.BlockSpec((places, tile), lambda i: (0, i)),
        out_shape=jax.ShapeDtypeStruct((places, columns), dtype),
        compiler_params=pltpu.CompilerParams(vmem_limit_bytes=VMEM),
        cost_estimate=QUICK,
        name="merge",
    )(matrix, *rows)


def ring_kernel(moves, given, *refs):
    ins, outs = refs[:given], refs[given:]
    for out, at, pieces in moves:
        first, start, rows, _ = pieces[0]
        value = ins[first][start : start + rows].astype(F32)
        for source, begin, count, offset in pieces[1:]:
            more = ins[source][begin : begin + count].astype(F32)
            if count < rows:
                sides = [value[:offset], value[offset + count :]]
                sides = [[jnp.zeros_like(side)] if side.shape[0] else [] for side in sides]
                more = jnp.concatenate([*sides[0], more, *sides[1]], axis=0)
            value = value + more
        outs[out][at : at + rows] = value.astype(BF)


def ring_step(inputs, moves, out_rows):
    columns = inputs[0][0].shape[1]
    tile = columns // 2
    return pl.pallas_call(
        functools.partial(ring_kernel, moves, len(inputs)),
        grid=(2,),
        in_specs=[
            pl.BlockSpec((rows, tile), functools.partial(lambda block, i: (block, i), block))
            for _, rows, block in inputs
        ],
        out_specs=[pl.BlockSpec((rows, tile), lambda i: (0, i)) for rows in out_rows],
        out_shape=[jax.ShapeDtypeStruct((rows, columns), BF) for rows in out_rows],
        compiler_params=pltpu.CompilerParams(vmem_limit_bytes=VMEM),
        cost_estimate=QUICK,
        name="ringstep",
    )(*[value for value, _, _ in inputs])


def last_kernel(done_ref, part_ref, ahead_ref, back_ref, out_ref):
    early = pl.program_id(0) < pl.num_programs(0) // 2

    @pl.when(early)
    def _():
        out_ref[...] = done_ref[...]

    @pl.when(jnp.logical_not(early))
    def _():
        total = part_ref[...] + ahead_ref[...].astype(F32) + back_ref[...].astype(F32)
        out_ref[...] = total.astype(BF)


def whole(value):
    return (value, value.shape[0], 0)


def rings(first, second, tokens, hold):
    half = tokens // 2

    def part(rest, apart):
        return (rest, tokens, ORDER.index(apart))

    def both(step, ahead, back):
        ahead, back = hold(step, [ahead, back])
        with jax.named_scope(f"step{step}"):
            return shift(ahead, dz=1), shift(back, dz=-1)

    def plain(rest, apart, ahead, back):
        return ring_step(
            [part(rest, apart), part(rest, NZ - apart), whole(ahead), whole(back)],
            [
                (0, 0, [(0, 0, tokens, 0), (2, 0, tokens, 0)]),
                (1, 0, [(1, 0, tokens, 0), (3, 0, tokens, 0)]),
            ],
            [tokens] * 2,
        )

    ahead, back = ring_step(
        [part(first, 4)], [(0, 0, [(0, 0, half, 0)]), (1, 0, [(0, half, half, 0)])], [half] * 2
    )
    ahead, back = both(1, ahead, back)
    ahead, back = ring_step(
        [part(first, 3), part(first, 5), whole(ahead), whole(back)],
        [
            (0, 0, [(0, 0, tokens, 0), (2, 0, half, 0)]),
            (1, 0, [(1, 0, tokens, 0), (3, 0, half, half)]),
        ],
        [tokens] * 2,
    )
    ahead, back = both(2, ahead, back)
    ahead, back = both(3, *plain(first, 2, ahead, back))
    later = second()
    ahead, back = ring_step(
        [part(first, 1), part(first, 7), part(later, 4), whole(ahead), whole(back)],
        [
            (0, 0, [(0, 0, tokens, 0), (3, 0, tokens, 0)]),
            (0, tokens, [(2, 0, half, 0)]),
            (1, 0, [(1, 0, tokens, 0), (4, 0, tokens, 0)]),
            (1, tokens, [(2, half, half, 0)]),
        ],
        [tokens + half] * 2,
    )
    ahead, back = both(4, ahead, back)
    done, ahead, back = ring_step(
        [part(first, 0), part(later, 3), part(later, 5), whole(ahead), whole(back)],
        [
            (1, 0, [(1, 0, tokens, 0), (3, tokens, half, 0)]),
            (2, 0, [(2, 0, tokens, 0), (4, tokens, half, half)]),
            (0, 0, [(0, 0, tokens, 0), (3, 0, tokens, 0), (4, 0, tokens, 0)]),
        ],
        [tokens] * 3,
    )
    ahead, back = both(5, ahead, back)
    ahead, back = both(6, *plain(later, 2, ahead, back))
    ahead, back = both(7, *plain(later, 1, ahead, back))
    columns = done.shape[1]
    tile, tiles = columns // 2, 2
    later_tile = lambda i: jnp.maximum(i - tiles, 0)
    return pl.pallas_call(
        last_kernel,
        grid=(2 * tiles,),
        in_specs=[
            pl.BlockSpec((tokens, tile), lambda i: (0, jnp.minimum(i, tiles - 1))),
            pl.BlockSpec((tokens, tile), lambda i: (ORDER.index(0), later_tile(i))),
        ]
        + [pl.BlockSpec((tokens, tile), lambda i: (0, later_tile(i)))] * 2,
        out_specs=pl.BlockSpec((tokens, tile), lambda i: (0, i)),
        out_shape=jax.ShapeDtypeStruct((tokens, 2 * columns), BF),
        compiler_params=pltpu.CompilerParams(vmem_limit_bytes=VMEM),
        cost_estimate=QUICK,
        name="last",
    )(done, later, ahead, back)


ROWS_FROM = (0, 1, 3, 2)
ORDER = (4, 3, 5, 2, 6, 1, 7, 0)
BEHIND = (0, -1, 1, -2, 2)


def holds(input_grad, taps_at):
    moved = {step: [taps_at[step - 1]] for step in (4, 5, 6)}
    return {2: [taps_at[1]], 3: [taps_at[2], input_grad]} | moved


def expert_part(
    routes,
    combine_weights,
    expert_rows,
    expert_weight,
    conv_grad,
    conv_input,
    conv_weight,
    tokens_total,
):
    me = lax.axis_index("expert")
    z, y, c = me // (NY * NC), (me // NC) % NY, me % NC
    capacity = expert_rows.shape[3]
    tokens, top = routes.shape
    block = capacity * NZ
    half = NY * block

    with jax.named_scope("sort"):
        rows = jnp.transpose(expert_rows[0, 0], (1, 0, 2))
        rows = sort_rows(rows, y, c)

    starts = [sum(WIDTHS[:chunk]) for chunk in range(len(WIDTHS))]

    with jax.named_scope("multiply"):
        out = jnp.dot(rows[half:], expert_weight[0], preferred_element_type=F32).astype(BF)
        kept = after(rows, out)[:half]
        kept = jnp.dot(kept, expert_weight[0], preferred_element_type=F32).astype(BF)
    with jax.named_scope("swap"):
        other = shift(out, dc=1)

    def ready(chunk, *first):
        with jax.named_scope(f"pack{chunk}"):
            return pack(after(kept, *first), other, starts[chunk], WIDTHS[chunk])

    def exchange(chunk, parts):
        with jax.named_scope(f"rows{chunk}"):
            return [parts[0]] + [shift(parts[apart], dy=apart) for apart in ROWS_FROM[1:]]

    count = len(WIDTHS)
    edges = conv_edges(after(conv_grad, rows), after(conv_input, rows))
    parts = [ready(0, *edges)]
    parts.append(ready(1, *parts[0][1:]))
    arrived = [exchange(0, parts[0])]
    begin = parts[0][1:]
    with jax.named_scope("info"):
        own = jnp.concatenate([routes.T.astype(F32), combine_weights.T], axis=0)[None]
        column = after(jnp.broadcast_to(own, (NZ, *own.shape[1:])), *begin)
        groups = [
            [device_at(place, row, core) for place in range(NZ)]
            for row in range(NY)
            for core in range(NC)
        ]
        column = lax.all_to_all(
            column, "expert", split_axis=0, concat_axis=0, tiled=True, axis_index_groups=groups
        )
    with jax.named_scope("gatescolumn"):
        matrix = column_matrix(me, column, ORDER, capacity)
    kernel = conv_taps(after(conv_weight, *begin))
    result, taps = conv_local(
        after(conv_grad, *begin), after(conv_input, *begin), edges, kernel
    )
    taps = taps_move(after(taps, column)) * (1.0 / math.sqrt(tokens_total))
    input_grad = conv_move(result)
    waited = [*arrived[0][1:], matrix, taps]
    arrived.append(exchange(1, [after(part, *waited) for part in parts[1]]))

    taps_at = [taps]
    for number, partner in enumerate(PARTNERS):
        with jax.named_scope(f"taps{number}"):
            taps_at.append(flip_sum(taps_at[-1], partner))

    first = merge_rows(matrix, [after(value, *parts[1][1:]) for value in arrived[0]], F32)

    def second():
        return merge_rows(matrix, arrived[1], F32)

    before = holds(input_grad, taps_at)

    def hold(step, values):
        return [after(value, *before[step]) for value in values] if step in before else values

    token_grad = rings(first, second, tokens, hold)
    return token_grad, input_grad, taps_at[-1]


def local(routes, combine_weights, expert_rows, expert_weight, conv_grad, conv_input, conv_weight):
    tokens_total = routes.shape[0] * lax.axis_size("expert") * lax.axis_size("seq")
    return expert_part(
        routes,
        combine_weights,
        expert_rows,
        expert_weight,
        conv_grad,
        conv_input,
        conv_weight,
        tokens_total,
    )


def solution(mesh):
    placed = (
        P(("expert", "seq"), None),
        P(("expert", "seq"), None),
        P("expert", "seq", None, None, None),
        P("expert", None, None),
        P(("expert", "seq"), None),
        P(("expert", "seq"), None),
        P(None, "seq"),
    )
    return jax.shard_map(
        local,
        mesh=mesh,
        in_specs=placed,
        out_specs=(P(("expert", "seq"), None), P("expert", "seq"), P(None, "seq")),
        check_vma=False,
    )
```
